256 devices in a mesh: replica: 8 (over x, z_hi), fsdp: 32 (over y, z_lo, core).
Axes of the slice: x: 4, y: 4, z: 8 (z_hi: 2, z_lo: 4; z = z_hi * 4 + z_lo), core: 2. Of those that a mesh axis runs over, the one named last changes fastest.
Arguments:
- acts: bfloat16 [65536, 2304], P(('replica', 'fsdp')), may hold values from -6 to 6
- value_weight: bfloat16 [2304, 1024], P('fsdp'), may hold values from -0.125 to 0.125
- out_weight: bfloat16 [1024, 2304], P('fsdp'), may hold values from -0.1875 to 0.1875
- norm_gain: float32 [2304], replicated, may hold values from 0.1 to 1.9
- cotan: bfloat16 [65536, 2304], P(('replica', 'fsdp')), may hold values from -6 to 6
Outputs:
- grad_value: float32 [2304, 1024], P('fsdp')
- grad_out: float32 [1024, 2304], P('fsdp')
- grad_acts: bfloat16 [65536, 2304], P(('replica', 'fsdp'))
The draws below stay inside these ranges and needn't reach their ends.
All inputs are finite; a program needn't handle non-finite values.
Results may differ from the reference program's by a relative error of at most 0.0059.
Values may be sent and summed in bfloat16 or wider, within the bound.
A program may use at most 64 MiB of HBM per device.

```python
import jax
import jax.numpy as jnp
from jax import lax

D = 2304
KVW = 1024
TOK_DEV = 256
TOKENS = 65536


def levels(key, dims, split, low, top_value):
    loudness = 1.0
    for axis_at, shards_of in split:
        steps = jax.random.uniform(jax.random.fold_in(jax.random.fold_in(key, 6), axis_at), (shards_of,), jnp.float32, low / len(split), top_value / len(split))
        loudness = loudness * jnp.repeat(jnp.exp(steps), dims[axis_at] // shards_of).reshape((-1,) + (1,) * (len(dims) - 1 - axis_at))
    return loudness


def bell_draw(rng, dims, deviation, limit, split=(), kind=jnp.bfloat16):
    drawn = jax.random.normal(rng, dims, jnp.float32) * deviation
    if len(split) > 0:
        drawn = levels(rng, dims, split, -0.22, 0.18) * drawn
    return jnp.clip(drawn, min=-limit, max=limit).astype(kind)


def setup_inputs(seed: int = 0) -> dict:
    streams_of = jax.random.split(jax.random.key(seed), 6)
    acts = bell_draw(streams_of[0], (TOKENS, D), 1.0, 6.0, ((0, 256),))
    value_weight = bell_draw(streams_of[1], (D, KVW), D ** -0.5, 0.125, ((0, 32),))
    out_weight = bell_draw(streams_of[2], (KVW, D), KVW ** -0.5, 0.1875, ((0, 32),))
    norm_gain = jnp.clip(1.0 + 0.18 * jax.random.normal(streams_of[3], (D,), jnp.float32), 0.1, 1.9)
    cotan = bell_draw(streams_of[4], (TOKENS, D), 1.0, 6.0, ((0, 256),))
    return dict(acts=acts, value_weight=value_weight, out_weight=out_weight, norm_gain=norm_gain, cotan=cotan)


def normalize(acts, norm_gain):
    xfloat = acts.astype(jnp.float32)
    inv_rms = lax.rsqrt(lax.optimization_barrier(jnp.mean(xfloat * xfloat, axis=-1, keepdims=True)) + 1e-06)
    normed = (xfloat * inv_rms * norm_gain).astype(jnp.bfloat16)
    return (xfloat, inv_rms, normed)

def block_sum(left, right):
    blocks = left.shape[0] // TOK_DEV
    left_b = left.reshape(blocks, TOK_DEV, left.shape[1])
    right_b = right.reshape(blocks, TOK_DEV, right.shape[1])

    def step(total, items):
        term = jnp.dot(items[0].T, items[1], preferred_element_type=jnp.float32)
        return (total + term, None)
    init = jnp.zeros((left.shape[1], right.shape[1]), jnp.float32)
    total, _ = lax.scan(step, init, (left_b, right_b))
    return total

def reference(acts, value_weight, out_weight, norm_gain, cotan):
    seqs = acts.shape[0] // TOK_DEV
    width = value_weight.shape[1]
    xfloat, inv_rms, normed = normalize(acts, norm_gain)
    values = jnp.dot(normed, value_weight, preferred_element_type=jnp.float32).astype(jnp.bfloat16)
    places = jnp.arange(TOK_DEV)
    lower_ones = (places[:, None] >= places[None, :]).astype(jnp.float32)
    counts = (places + 1).astype(jnp.float32)[:, None]
    seq_values = values.astype(jnp.float32).reshape(seqs, TOK_DEV, width)
    summed = jnp.einsum('st,btk->bsk', lower_ones, seq_values, precision=lax.Precision.HIGHEST)
    mixed = (summed / counts).reshape(seqs * TOK_DEV, width).astype(jnp.bfloat16)
    back = jnp.dot(cotan, out_weight.T, preferred_element_type=jnp.float32)
    dmix = (back.reshape(seqs, TOK_DEV, width) / counts).astype(jnp.bfloat16)
    dvalues = jnp.einsum('st,bsk->btk', lower_ones, dmix.astype(jnp.float32), precision=lax.Precision.HIGHEST)
    dvalues = dvalues.reshape(seqs * TOK_DEV, width).astype(jnp.bfloat16)
    grad_out = block_sum(mixed, cotan)
    grad_value = block_sum(normed, dvalues)
    dnormed = jnp.dot(dvalues, value_weight.T, preferred_element_type=jnp.float32)
    scaled = norm_gain * dnormed
    dyf = cotan.astype(jnp.float32)
    moment = lax.optimization_barrier(jnp.mean(scaled * xfloat, axis=-1, keepdims=True))
    grad_acts = dyf + inv_rms * scaled - xfloat * inv_rms * inv_rms * inv_rms * moment
    return (grad_value, grad_out, grad_acts.astype(jnp.bfloat16))
```

```python
import functools

import jax
import jax.numpy as jnp
from jax import lax
from jax.experimental import pallas as pl
from jax.experimental.pallas import tpu as pltpu
from jax.sharding import PartitionSpec as P

MESH = pl.DeviceIdType.MESH
BF, F32 = jnp.bfloat16, jnp.float32
D, KVW, TOK = 2304, 1024, 256
HALF_D, HALF_K = D // 2, KVW // 2
N_SEM = 144


def nt(a, b):
    return lax.dot_general(a, b, (((1,), (1,)), ((), ())), preferred_element_type=F32)


def nn(a, b):
    return jnp.dot(a, b, preferred_element_type=F32)


def loop(n, body):
    def step(i, carry):
        body(i)
        return carry

    lax.fori_loop(0, n, step, 0)


def rows(ref, start, size):
    return ref.at[pl.ds(pl.multiple_of(start, 16), size)]


def kernel(
    acts, wv, wo, gain, cotan,
    gv_out, go_out, ga_out,
    cot2, nrm, nrm2, nrmt, inv_ref, wo_a, wo_b, wv_a, wv_b, wvx,
    dmix, dval, vals, mix_t, mix_tb,
    gvq, gx0, gx1, gxl, gxr, gvu, gy0, gy1, gyl, gyr, gvv, gz0, gz1, gzl, gzr, gvw, gvw2, gvf, gvx, gvo,
    go_a, go_b, a0, a1, al, ar, qa, az0, az1, azl, azr,
    b0, b1, bl, br, qb, by0, by1, byl, byr, gos, gosr, got, got2, gof,
    dn_own, dn_send, dn_recv,
    ssem, rsem,
):
    r, f = lax.axis_index("replica"), lax.axis_index("fsdp")
    x, y, zl, c = r // 2, f // 8, (f // 2) % 4, f % 2
    z = (r % 2) * 4 + zl

    def dev(dx=0, dy=0, dz=0, dc=0):
        xx, yy, zz, cc = (x + dx + 4) % 4, (y + dy + 4) % 4, (z + dz + 8) % 8, (c + dc) % 2
        return (xx * 2 + zz // 4, yy * 8 + (zz % 4) * 2 + cc)

    def ydev(s):
        return dev(dy=s)

    def zdev(s):
        return dev(dz=s)

    def xdev(s):
        return dev(dx=s)

    def at4(q, s):
        return (q + s + 4) % 4

    core = dev(dc=1)
    partners = [core, xdev(1), xdev(-1), xdev(2), ydev(1), ydev(-1), zdev(1), zdev(-1), zdev(4)]
    barrier = pltpu.get_barrier_semaphore()
    for p in partners:
        pl.semaphore_signal(barrier, inc=1, device_id=p, device_id_type=MESH)
    pl.semaphore_wait(barrier, len(partners))

    sent = []

    def send(src, dst, to):
        i = len(sent)
        copy = pltpu.make_async_remote_copy(
            src_ref=src, dst_ref=dst, send_sem=ssem.at[i], recv_sem=rsem.at[i],
            device_id=to, device_id_type=MESH,
        )
        copy.start()
        sent.append(copy)
        return copy

    class Gather:
        def __init__(self, buf, size, cut, first, second, slot):
            self.buf, self.size, self.cut = buf, size, cut
            self.first, self.second, self.slot = first, second, slot
            self.p2, self.fw = {}, {}

        def block(self, i, j, half=None):
            start = self.slot(i, j) * self.size
            if half is None:
                return rows(self.buf, start, self.size)
            if half == 0:
                return rows(self.buf, start, self.cut)
            return rows(self.buf, start + self.cut, self.size - self.cut)

        def own(self):
            b = self.block(0, 0)
            self.p1p = send(b, b, self.first(1))
            self.p1m = send(b, b, self.first(-1))
            self.chunk(0)

        def chunk(self, i):
            b = self.block(i, 0)
            self.p2[i] = (send(b, b, self.second(1)), send(b, b, self.second(-1)))

        def near(self):
            self.p1p.wait_recv()
            b = self.block(-1, 0, 0)
            self.f1p = send(b, b, self.first(1))
            self.p1m.wait_recv()
            b = self.block(1, 0, 1)
            self.f1m = send(b, b, self.first(-1))
            self.chunk(-1)
            self.chunk(1)

        def far(self):
            self.f1p.wait_recv()
            self.f1m.wait_recv()
            self.chunk(2)

        def forward(self, i):
            up, down = self.p2[i]
            up.wait_recv()
            b = self.block(i, -1, 0)
            fu = send(b, b, self.second(1))
            down.wait_recv()
            b = self.block(i, 1, 1)
            fd = send(b, b, self.second(-1))
            self.fw[i] = (fu, fd)

        def finish(self):
            for i in (0, -1, 1, 2):
                self.fw[i][0].wait_recv()
                self.fw[i][1].wait_recv()

    def slot_yz(i, j):
        return at4(y, i) * 4 + at4(zl, j)

    def slot_zy(i, j):
        return at4(y, j) * 4 + at4(zl, i)

    class Scatter:
        def __init__(self, part, n, cut, to, q, f0, f1, left, right):
            self.part, self.n, self.cut, self.to, self.q = part, n, cut, to, q
            self.f0, self.f1, self.left, self.right = f0, f1, left, right

        def half(self, s, h):
            start = at4(self.q, s) * self.n
            if h == 0:
                return rows(self.part, start, self.cut)
            return rows(self.part, start + self.cut, self.n - self.cut)

        def open(self):
            n, k = self.n, self.cut
            self.c0 = send(self.half(2, 0), self.f0, self.to(1))
            self.c1 = send(self.half(2, 1), self.f1, self.to(-1))
            self.l1 = send(self.half(1, 1), self.left.at[pl.ds(k, n - k)], self.to(1))
            self.r0 = send(self.half(-1, 0), self.right.at[pl.ds(0, k)], self.to(-1))

        def turn(self):
            n, k = self.n, self.cut
            self.c0.wait_recv()
            h = self.half(1, 0)
            h[...] = (h[...].astype(F32) + self.f0[...].astype(F32)).astype(BF)
            self.l0 = send(h, self.left.at[pl.ds(0, k)], self.to(1))
            self.c1.wait_recv()
            h = self.half(-1, 1)
            h[...] = (h[...].astype(F32) + self.f1[...].astype(F32)).astype(BF)
            self.r1 = send(h, self.right.at[pl.ds(k, n - k)], self.to(-1))

        def close(self, out):
            for copy in (self.l1, self.r0, self.l0, self.r1):
                copy.wait_recv()
            mine = rows(self.part, self.q * self.n, self.n)
            total = mine[...].astype(F32) + self.left[...].astype(F32) + self.right[...].astype(F32)
            out[...] = total.astype(BF).reshape(out.shape)

    me = y * 4 + zl
    rows(wo_a, me * 32, 32)[...] = wo[:, :HALF_D]
    rows(wo_b, me * 32, 32)[...] = wo[:, HALF_D:]
    ga = Gather(wo_a, 32, 16, ydev, zdev, slot_yz)
    gb = Gather(wo_b, 32, 16, zdev, ydev, slot_zy)
    ga.own()
    gb.own()
    cot_copy = send(cotan, cot2, core)

    jj = lax.broadcasted_iota(jnp.int32, (128, 256), 0)
    kk = lax.broadcasted_iota(jnp.int32, (128, 256), 1)
    base = 64 * (jj // 32) + jj % 32

    def picks(which):
        return (kk == base + 32 * which).astype(BF)

    pick_own, pick_other = picks(c), picks(1 - c)
    own_rows = pl.ds(pl.multiple_of(c * 72, 8), 72)
    for q in range(4):
        group = wv[:, 256 * q : 256 * (q + 1)]
        gvx[:, 128 * q : 128 * (q + 1)] = nt(group, pick_other)
        wvx[own_rows, 128 * q : 128 * (q + 1)] = nt(group, pick_own)
    wvx_copy = send(gvx, wvx.at[own_rows], core)

    def norm_step(i):
        at = pl.ds(pl.multiple_of(i * 32, 32), 32)
        xf = acts[at, :].astype(F32)
        inv = lax.rsqrt(jnp.mean(xf * xf, axis=-1, keepdims=True) + 1e-06)
        inv_ref[at, :] = inv
        nrm[at, :] = (xf * inv * gain[...]).astype(BF)

    loop(8, norm_step)
    nrm_copy = send(nrm, nrm2, core)

    ga.near()
    gb.near()
    ga.forward(0)
    gb.forward(0)
    ga.far()
    gb.far()
    for i in (-1, 1):
        ga.forward(i)
        gb.forward(i)

    wvx_copy.wait_recv()
    rows(wv_a, me * 144, 144)[...] = wvx[:, :256].astype(BF)
    rows(wv_b, me * 144, 144)[...] = wvx[:, 256:].astype(BF)
    va = Gather(wv_a, 144, 80, ydev, zdev, slot_yz)
    vb = Gather(wv_b, 144, 80, zdev, ydev, slot_zy)
    ga.forward(2)
    gb.forward(2)
    va.own()
    vb.own()

    def turn_step(src, at):
        def body(t):
            lanes = pl.ds(pl.multiple_of(t * 256, 256), 256)
            nrmt[lanes, at * 256 : (at + 1) * 256] = src[:, lanes].T

        return body

    loop(9, turn_step(nrm, 0))
    nrm_copy.wait_recv()
    loop(9, turn_step(nrm2, 1))
    cot_copy.wait_recv()
    ga.finish()
    gb.finish()

    ri = lax.broadcasted_iota(jnp.int32, (TOK, TOK), 0)
    ci = lax.broadcasted_iota(jnp.int32, (TOK, TOK), 1)
    lower = (ri >= ci).astype(BF)
    upper = (ci >= ri).astype(BF)
    per_count = 1.0 / (lax.broadcasted_iota(jnp.int32, (TOK, 1), 0) + 1).astype(F32)

    for s, cot in enumerate((cotan, cot2)):

        def dmix_step(n, cot=cot, s=s):
            at = pl.ds(pl.multiple_of(n * 256, 256), 256)
            d = nt(cot[:, :HALF_D], wo_a[at, :]) + nt(cot[:, HALF_D:], wo_b[at, :])
            dmix[:, at] = (d * per_count).astype(BF)

        loop(2, dmix_step)
        dval[256 * s : 256 * (s + 1), :] = nn(upper, dmix[...]).astype(BF)
        if s == 0:
            va.near()
            vb.near()

    va.forward(0)
    vb.forward(0)
    va.far()
    vb.far()

    def gv_step(t):
        at = pl.ds(pl.multiple_of(t * 256, 256), 256)
        g = nn(nrmt[at, :], dval[...])
        for q in range(4):
            gvq[pl.ds(pl.multiple_of(q * D + t * 256, 256), 256), :] = g[:, 128 * q : 128 * (q + 1)].astype(BF)

    loop(9, gv_step)
    gvx_rs = Scatter(gvq, D, D // 2, xdev, x, gx0, gx1, gxl, gxr)
    gvx_rs.open()

    for i in (-1, 1, 2):
        va.forward(i)
        vb.forward(i)
    va.finish()
    vb.finish()

    for s, nr in enumerate((nrm, nrm2)):
        vals[:, :256] = nn(nr[...], wv_a[...]).astype(BF)
        vals[:, 256:] = nn(nr[...], wv_b[...]).astype(BF)
        mixed = (nn(lower, vals[...]) * per_count).astype(BF)
        mix_t[:, 256 * s : 256 * (s + 1)] = mixed.T
    for m in range(16):
        yy, zz = m // 4, m % 4
        n = 4 * zz + yy
        mix_tb[32 * n : 32 * (n + 1), :] = mix_t[32 * m : 32 * (m + 1), :]
    for src, dst, lo in ((mix_t, go_a, 0), (mix_tb, go_b, HALF_D)):

        def go_step(n, src=src, dst=dst, lo=lo):
            at = pl.ds(pl.multiple_of(n * 256, 256), 256)
            g = nn(src[at, :256], cotan[:, lo : lo + HALF_D]) + nn(src[at, 256:], cot2[:, lo : lo + HALF_D])
            dst[at, :] = g.astype(BF)

        loop(2, go_step)

    oa = Scatter(go_a, 128, 64, ydev, y, a0, a1, al, ar)
    ob = Scatter(go_b, 128, 64, zdev, zl, b0, b1, bl, br)
    oa.open()
    ob.open()
    gvx_rs.turn()

    def dn_step(t):
        at = pl.ds(pl.multiple_of(t * 256, 256), 256)
        d = nt(dval[:, :256], wv_a[at, :]) + nt(dval[:, 256:], wv_b[at, :])
        dn_own[:, at] = d[:256]
        dn_send[:, at] = d[256:].astype(BF)

    loop(9, dn_step)
    dn_copy = send(dn_send, dn_recv, core)
    oa.turn()
    ob.turn()

    gvx_rs.close(gvu)
    gvy_rs = Scatter(gvu, 576, 288, ydev, y, gy0, gy1, gyl, gyr)
    gvy_rs.open()

    dn_copy.wait_recv()

    def ga_step(i):
        at = pl.ds(pl.multiple_of(i * 32, 32), 32)
        xf, inv = acts[at, :].astype(F32), inv_ref[at, :]
        scaled = gain[...] * (dn_own[at, :] + dn_recv[at, :].astype(F32))
        moment = jnp.mean(scaled * xf, axis=-1, keepdims=True)
        out = cotan[at, :].astype(F32) + inv * scaled - xf * (inv * inv * inv * moment)
        ga_out[at, :] = out.astype(BF)

    loop(8, ga_step)

    oa.close(qa)
    oaz = Scatter(qa, 32, 16, zdev, zl, az0, az1, azl, azr)
    oaz.open()
    ob.close(qb)
    oby = Scatter(qb, 32, 16, ydev, y, by0, by1, byl, byr)
    oby.open()
    gvy_rs.turn()
    oaz.turn()
    oby.turn()
    gvy_rs.close(gvv)
    gvz_rs = Scatter(gvv, 144, 80, zdev, zl, gz0, gz1, gzl, gzr)
    gvz_rs.open()

    oaz.close(gos.at[0:2])
    oby.close(gos.at[2:4])
    cx = [send(gos.at[at4(x, s)], gosr.at[n], xdev(s)) for n, s in enumerate((1, -1, 2))]
    gvz_rs.turn()
    for copy in cx:
        copy.wait_recv()
    t = gos[x].astype(F32) + gosr[0].astype(F32) + gosr[1].astype(F32) + gosr[2].astype(F32)
    got[...] = t.astype(BF)
    ct = send(got, got2, zdev(4))
    gvz_rs.close(gvw)
    cw = send(gvw, gvw2, zdev(4))
    ct.wait_recv()
    gof[x] = (got[...].astype(F32) + got2[...].astype(F32)).astype(BF)
    co = [send(gof.at[x], gof.at[x], xdev(s)) for s in (1, -1, 2)]
    cw.wait_recv()
    gvf[x] = (gvw[...].astype(F32) + gvw2[...].astype(F32)).astype(BF)
    cv = [send(gvf.at[x], gvf.at[x], xdev(s)) for s in (1, -1, 2)]
    for copy in co:
        copy.wait_recv()
    for h in range(2):
        go_out[0:16, HALF_D * h : HALF_D * (h + 1)] = gof[2 * h].astype(F32)
        go_out[16:32, HALF_D * h : HALF_D * (h + 1)] = gof[2 * h + 1].astype(F32)
    for copy in cv:
        copy.wait_recv()
    for q in range(4):
        gvo[0:144, 128 * q : 128 * (q + 1)] = gvf[q].astype(F32)
    cg = send(gvo.at[pl.ds(pl.multiple_of((1 - c) * 72, 8), 72)], gvo.at[pl.ds(144, 72)], core)
    cg.wait_recv()
    for q in range(4):
        lanes = slice(128 * q, 128 * (q + 1))
        own = gvo[own_rows, lanes].astype(BF)
        other = gvo[144:216, lanes].astype(BF)
        gv_out[:, 256 * q : 256 * (q + 1)] = nn(own, pick_own) + nn(other, pick_other)

    for copy in sent:
        copy.wait_send()


def local(acts, value_weight, out_weight, norm_gain, cotan):
    vmem = pl.BlockSpec(memory_space=pltpu.VMEM)

    def bf(*shape):
        return pltpu.VMEM(shape, BF)

    def fl(*shape):
        return pltpu.VMEM(shape, F32)

    scratch = [
        bf(TOK, D), bf(TOK, D), bf(TOK, D), bf(D, 2 * TOK), fl(TOK, 1),
        bf(HALF_K, HALF_D), bf(HALF_K, HALF_D), bf(D, 256), bf(D, 256), fl(144, HALF_K),
        bf(TOK, HALF_K), bf(2 * TOK, HALF_K), bf(TOK, HALF_K), bf(HALF_K, 2 * TOK), bf(HALF_K, 2 * TOK),
        bf(4 * D, 128), bf(1152, 128), bf(1152, 128), bf(D, 128), bf(D, 128),
        bf(D, 128), bf(288, 128), bf(288, 128), bf(576, 128), bf(576, 128),
        bf(576, 128), bf(80, 128), bf(64, 128), bf(144, 128), bf(144, 128),
        bf(144, 128), bf(144, 128), bf(4, 144, 128), fl(72, HALF_K), fl(216, HALF_K),
        bf(HALF_K, HALF_D), bf(HALF_K, HALF_D),
        bf(64, HALF_D), bf(64, HALF_D), bf(128, HALF_D), bf(128, HALF_D),
        bf(128, HALF_D), bf(16, HALF_D), bf(16, HALF_D), bf(32, HALF_D), bf(32, HALF_D),
        bf(64, HALF_D), bf(64, HALF_D), bf(128, HALF_D), bf(128, HALF_D),
        bf(128, HALF_D), bf(16, HALF_D), bf(16, HALF_D), bf(32, HALF_D), bf(32, HALF_D),
        bf(4, 16, HALF_D), bf(3, 16, HALF_D), bf(16, HALF_D), bf(16, HALF_D), bf(4, 16, HALF_D),
        fl(TOK, D), bf(TOK, D), bf(TOK, D),
        pltpu.SemaphoreType.DMA((N_SEM,)), pltpu.SemaphoreType.DMA((N_SEM,)),
    ]
    return pl.pallas_call(
        kernel,
        out_shape=(
            jax.ShapeDtypeStruct((72, KVW), F32),
            jax.ShapeDtypeStruct((32, D), F32),
            jax.ShapeDtypeStruct((TOK, D), BF),
        ),
        in_specs=[vmem] * 5,
        out_specs=(vmem, vmem, vmem),
        scratch_shapes=scratch,
        name="fused",
        compiler_params=pltpu.CompilerParams(
            collective_id=0, has_side_effects=True, vmem_limit_bytes=56 * 2**20
        ),
    )(acts, value_weight, out_weight, norm_gain.reshape(1, D), cotan)


def solution(mesh):
    placed = (
        P(("replica", "fsdp"), None),
        P("fsdp", None),
        P("fsdp", None),
        P(),
        P(("replica", "fsdp"), None),
    )
    return jax.shard_map(
        local,
        mesh=mesh,
        in_specs=placed,
        out_specs=(P("fsdp", None), P("fsdp", None), P(("replica", "fsdp"), None)),
        check_vma=False,
    )
```

```python
import math

import jax
import jax.numpy as jnp
from jax import lax
from jax.experimental import pallas as pl
from jax.experimental.pallas import tpu as pltpu
from jax.sharding import PartitionSpec as P

MESH = pl.DeviceIdType.MESH
BF, F32 = jnp.bfloat16, jnp.float32
D, KVW, TOK = 2304, 1024, 256
HALF_D, HALF_K = D // 2, KVW // 2
N_OUT, N_IN = 12, 96
TALLY = 9216


def nt(a, b):
    return lax.dot_general(a, b, (((1,), (1,)), ((), ())), preferred_element_type=F32)


def nn(a, b):
    return jnp.dot(a, b, preferred_element_type=F32)


def loop(n, body):
    def step(i, carry):
        body(i)
        return carry

    lax.fori_loop(0, n, step, 0)


def rows(ref, start, size):
    return ref.at[pl.ds(pl.multiple_of(start, 16), size)]


def kernel(*refs):
    ref = dict(zip(("acts_in", "wv_in", "wo_in", "gain", "cot_in", "gv_out", "go_out", "ga_hbm", *SCRATCH), refs))
    acts_in, wv_in, wo_in, gain, cot_in = (ref[n] for n in ("acts_in", "wv_in", "wo_in", "gain", "cot_in"))
    gv_out, go_out, ga_hbm = (ref[n] for n in ("gv_out", "go_out", "ga_hbm"))
    acts, wv, cotan, cot2, nrm, nrm2, nrmt, inv_ref, wo_a, wo_b, wvf, wvx, wvs = (ref[n] for n in INPUTS)
    dmix, dval, vals, mix_t, mix_tb, dn_own, dn_send, dn_recv, ga_out, tally = (ref[n] for n in WORK)
    gvw, gvw2, fin, got, got2, gof, ssem, rsem, lsem = (ref[n] for n in LAST)
    r, f = lax.axis_index("replica"), lax.axis_index("fsdp")
    x, y, zl, c = r // 2, f // 8, (f // 2) % 4, f % 2
    z = (r % 2) * 4 + zl
    me = y * 4 + zl

    def dev(dx=0, dy=0, dz=0, dc=0):
        xx, yy, zz, cc = (x + dx + 4) % 4, (y + dy + 4) % 4, (z + dz + 8) % 8, (c + dc) % 2
        return (xx * 2 + zz // 4, yy * 8 + (zz % 4) * 2 + cc)

    def ydev(s):
        return dev(dy=s)

    def zdev(s):
        return dev(dz=s)

    def xdev(s):
        return dev(dx=s)

    def at4(q, s):
        return (q + s + 4) % 4

    own_wo = [
        pltpu.make_async_copy(wo_in.at[:, pl.ds(HALF_D * h, HALF_D)], rows(buf, me * 32, 32), lsem.at[h])
        for h, buf in enumerate((wo_a, wo_b))
    ]
    own_wv = pltpu.make_async_copy(wv_in, wv, lsem.at[2])
    own_cot = pltpu.make_async_copy(cot_in, cotan, lsem.at[3])
    own_acts = pltpu.make_async_copy(acts_in, acts, lsem.at[4])
    for copy in (*own_wo, own_wv, own_cot, own_acts):
        copy.start()

    core = dev(dc=1)
    partners = [core, *(xdev(s) for s in (1, -1, 2)), *(dev(dx=s, dc=1) for s in (1, -1, 2))]
    partners += [*(ydev(s) for s in (1, -1, 2)), *(zdev(s) for s in (1, -1, 2, -2, 4))]
    barrier = pltpu.get_barrier_semaphore()
    for p in partners:
        pl.semaphore_signal(barrier, inc=1, device_id=p, device_id_type=MESH)
    pl.semaphore_wait(barrier, len(partners))

    def await_bytes(n, sem):
        view = tally.at[pl.ds(0, n // 256)]
        pltpu.make_async_copy(view, view, sem).wait()

    out_bytes, in_count = [0], [0]

    class Group:
        def __init__(self):
            self.i, self.bytes = in_count[0], 0
            in_count[0] += 1

        def wait(self):
            await_bytes(self.bytes, rsem.at[self.i])

    def send(src, dst, to, group=None):
        n = math.prod(src.shape) * jnp.dtype(src.dtype).itemsize
        if out_bytes[-1] + n > TALLY * 256:
            out_bytes.append(0)
        out_bytes[-1] += n
        alone = group is None
        group = Group() if alone else group
        group.bytes += n
        copy = pltpu.make_async_remote_copy(
            src_ref=src, dst_ref=dst, send_sem=ssem.at[len(out_bytes) - 1], recv_sem=rsem.at[group.i],
            device_id=to, device_id_type=MESH,
        )
        copy.start()
        return copy if alone else None

    class Gather:
        def __init__(self, first, second, block):
            self.first, self.second, self.block = first, second, block
            self.p2, self.rest = {}, Group()

        def spread(self, to, block, near, far):
            b = block(None)
            copies = (send(b, b, to(1), near), send(b, b, to(-1), near))
            if to is zdev:
                h0, h1 = block(0), block(1)
                send(h0, h0, to(2), far)
                send(h1, h1, to(-2), far)
            else:
                send(b, b, to(2), far)
            return copies

        def own(self):
            self.p1far = Group()
            self.p1 = self.spread(self.first, lambda h: self.block(0, 0, h), None, self.p1far)

        def chunk(self, i):
            b = self.block(i, 0, None)
            self.p2[i] = (send(b, b, self.second(1)), send(b, b, self.second(-1)))

        def direct(self, i):
            self.spread(self.second, lambda h: self.block(i, 0, h), self.rest, self.rest)

        def near(self, then):
            self.p1[0].wait_recv()
            then(-1)
            self.p1[1].wait_recv()
            then(1)

        def far(self, then):
            self.p1far.wait()
            then(2)

        def forward(self, i):
            up, down = self.p2[i]
            up.wait_recv()
            b = self.block(i, -1, 0)
            send(b, b, self.second(1), self.rest)
            down.wait_recv()
            b = self.block(i, 1, 1)
            send(b, b, self.second(-1), self.rest)

        def finish(self):
            self.rest.wait()

    def slot_yz(i, j):
        return at4(y, i) * 4 + at4(zl, j)

    def slot_zy(i, j):
        return at4(y, j) * 4 + at4(zl, i)

    def wo_block(buf, slot):
        def block(i, j, half):
            start = slot(i, j) * 32
            if half is None:
                return rows(buf, start, 32)
            return rows(buf, start + 16 * half, 16)

        return block

    def wv_block(slot, lo, n):
        def block(i, j, half):
            at = wvf.at[slot(i, j), pl.ds(lo, n)]
            return at if half is None else at.at[:, pl.ds(256 * half, 256)]

        return block

    def wv_shared(i, j, half):
        at = wvf.at[slot_zy(i, j), pl.ds(pl.multiple_of(16 * x, 16), 16)]
        return at if half is None else at.at[:, pl.ds(256 * half, 256)]

    class Ring:
        def __init__(self, to, part, f0, f1, left, right):
            self.to, self.part = to, part
            self.f0, self.f1, self.left, self.right = f0, f1, left, right

        def recv(self, ref, h):
            return ref.at[pl.ds(2 * h, 2)]

        def open(self):
            self.rest = Group()
            self.c0 = send(self.part(2, 0), self.f0, self.to(1))
            self.c1 = send(self.part(2, 1), self.f1, self.to(-1))
            send(self.part(1, 1), self.recv(self.left, 1), self.to(1), self.rest)
            send(self.part(-1, 0), self.recv(self.right, 0), self.to(-1), self.rest)

        def turn(self):
            self.c0.wait_recv()
            h = self.part(1, 0)
            h[...] = (h[...].astype(F32) + self.f0[...].astype(F32)).astype(BF)
            send(h, self.recv(self.left, 0), self.to(1), self.rest)
            self.c1.wait_recv()
            h = self.part(-1, 1)
            h[...] = (h[...].astype(F32) + self.f1[...].astype(F32)).astype(BF)
            send(h, self.recv(self.right, 1), self.to(-1), self.rest)

        def close(self, out):
            self.rest.wait()
            for h in range(2):
                total = self.part(0, h)[...].astype(F32) + self.recv(self.left, h)[...].astype(F32)
                total += self.recv(self.right, h)[...].astype(F32)
                o = self.recv(out, h)
                o[...] = total.astype(BF)

    class Direct:
        def __init__(self, to, part, left, right, far, halves):
            self.part, self.left, self.right, self.far = part, left, right, far
            self.group = Group()
            send(part(1), left, to(1), self.group)
            send(part(-1), right, to(-1), self.group)
            p = part(2)
            if to is zdev:
                for h, hop in enumerate((2, -2)):
                    send(halves(p, h), halves(far, h), to(hop), self.group)
            else:
                send(p, far, to(2), self.group)

        def close(self, out):
            self.group.wait()
            total = self.part(0)[...].astype(F32) + self.left[...].astype(F32)
            total += self.right[...].astype(F32) + self.far[...].astype(F32)
            out[...] = total.astype(BF)

    def two(p, h):
        return p.at[pl.ds(2 * h, 2)]

    class Reduce:
        def __init__(self, name, halves, outs):
            self.bufs = [[ref[f"{name}{p}_{n}"] for n in PART] for p in range(3)]
            self.halves, self.outs = halves, outs
            bx, by, bz = (b[0] for b in self.bufs)
            self.parts = (
                (xdev, lambda s, h: bx.at[at4(x, s), pl.ds(2 * h, 2)]),
                (ydev, lambda s, h: by.at[pl.ds(2 * h, 2), at4(y, s)]),
                (zdev, lambda s, h: bz.at[pl.ds(2 * h, 2), :, at4(zl, s)]),
            )
            self.rings = [None] * 3

        def open(self, p):
            self.rings[p] = Ring(*self.parts[p], *self.bufs[p][1:5])
            self.rings[p].open()

        def turn(self, p):
            self.rings[p].turn()

        def second(self, p):
            done = self.bufs[p][5]
            self.rings[p].close(done)
            to, part = (
                (ydev, lambda s: done.at[at4(y, s)]),
                (zdev, lambda s: done.at[:, at4(zl, s)]),
                (xdev, lambda s: done.at[at4(x, s)]),
            )[p]
            self.rings[p] = Direct(to, part, *self.bufs[p][6:9], two)

        def third(self, p):
            done = self.bufs[p][9]
            self.rings[p].close(done)
            to, q = ((zdev, zl), (xdev, x), (ydev, y))[p]
            self.rings[p] = Direct(to, lambda s: done.at[at4(q, s)], *self.bufs[p][10:13], self.halves)

        def close(self):
            for p in range(3):
                self.rings[p].close(self.outs(p))

    ga = Gather(ydev, zdev, wo_block(wo_a, slot_yz))
    gb = Gather(zdev, ydev, wo_block(wo_b, slot_zy))
    for copy in own_wo:
        copy.wait()
    ga.own()
    gb.own()
    ga.chunk(0)
    gb.chunk(0)

    jj = lax.broadcasted_iota(jnp.int32, (128, 256), 0)
    kk = lax.broadcasted_iota(jnp.int32, (128, 256), 1)
    base = 64 * (jj // 32) + jj % 32

    def picks(which):
        return (kk == base + 32 * which).astype(BF)

    pick_own, pick_other = picks(c), picks(1 - c)
    own_rows = pl.ds(pl.multiple_of(c * 72, 8), 72)
    own_wv.wait()
    for q in range(4):
        group = wv[:, 256 * q : 256 * (q + 1)]
        wvs[:, 128 * q : 128 * (q + 1)] = nt(group, pick_other)
    wvx_copy = send(wvs, wvx.at[own_rows], core)
    for q in range(4):
        group = wv[:, 256 * q : 256 * (q + 1)]
        wvx[own_rows, 128 * q : 128 * (q + 1)] = nt(group, pick_own)
    own_cot.wait()
    cot_copy = send(cotan, cot2, core)

    own_acts.wait()

    def norm_step(i):
        at = pl.ds(pl.multiple_of(i * 32, 32), 32)
        xf = acts[at, :].astype(F32)
        inv = lax.rsqrt(jnp.mean(xf * xf, axis=-1, keepdims=True) + 1e-06)
        inv_ref[at, :] = inv
        nrm[at, :] = (xf * inv * gain[...].reshape(1, D)).astype(BF)

    loop(8, norm_step)
    nrm_copy = send(nrm, nrm2, core)

    wvx_copy.wait_recv()
    mine = pl.ds(pl.multiple_of(16 * x, 16), 16)
    wvf[me, mine] = wvx[mine, :].astype(BF)
    wvf[me, 64:144] = wvx[64:144].astype(BF)
    vs = Gather(zdev, ydev, wv_shared)
    vs.own()
    vs.direct(0)
    ga.near(ga.chunk)
    gb.near(gb.chunk)
    ga.far(ga.chunk)
    gb.far(gb.chunk)
    ga.forward(0)
    gb.forward(0)
    vs.near(vs.direct)
    vs.far(vs.direct)
    for i in (-1, 1, 2):
        ga.forward(i)
        gb.forward(i)
    va = Gather(ydev, zdev, wv_block(slot_yz, 64, 48))
    vb = Gather(zdev, ydev, wv_block(slot_zy, 112, 32))
    va.own()
    vb.own()
    va.chunk(0)
    vb.chunk(0)

    def turn_step(src, at):
        def body(t):
            lanes = pl.ds(pl.multiple_of(t * 256, 256), 256)
            nrmt[lanes, at * 256 : (at + 1) * 256] = src[:, lanes].T

        return body

    loop(9, turn_step(nrm, 0))
    nrm_copy.wait_recv()
    vs.finish()
    share = wvf.at[:, pl.ds(pl.multiple_of(16 * x, 16), 16)]
    vx = (send(share, share, xdev(1)), send(share, share, xdev(-1)))
    loop(9, turn_step(nrm2, 1))
    cot_copy.wait_recv()
    va.near(va.chunk)
    vb.near(vb.chunk)
    va.far(va.chunk)
    vb.far(vb.chunk)
    ga.finish()
    gb.finish()

    ri = lax.broadcasted_iota(jnp.int32, (TOK, TOK), 0)
    ci = lax.broadcasted_iota(jnp.int32, (TOK, TOK), 1)
    lower = (ri >= ci).astype(BF)
    upper = (ci >= ri).astype(BF)
    per_count = 1.0 / (lax.broadcasted_iota(jnp.int32, (TOK, 1), 0) + 1).astype(F32)

    for s, cot in enumerate((cotan, cot2)):

        def dmix_step(n, cot=cot, s=s):
            at = pl.ds(pl.multiple_of(n * 256, 256), 256)
            d = nt(cot[:, :HALF_D], wo_a[at, :]) + nt(cot[:, HALF_D:], wo_b[at, :])
            dmix[:, at] = (d * per_count).astype(BF)

        loop(2, dmix_step)
        dval[256 * s : 256 * (s + 1), :] = nn(upper, dmix[...]).astype(BF)
        if s == 0:
            va.forward(0)
            vb.forward(0)

    gv = Reduce("gv", lambda p, h: p.at[pl.ds(32 * h, 32 - 16 * h)], lambda p: gvw.at[pl.ds(48 * p, 48)])

    def gv_half(p):
        def body(t):
            at = pl.ds(pl.multiple_of(t * 576, 16), 576)
            g = nn(nrmt[at, :], dval[:, 256 * p : 256 * (p + 1)]).astype(BF)
            for h in range(2):
                block = g[:, 128 * h : 128 * (h + 1)].reshape(4, 144, 128)
                for k in range(3):
                    gv.bufs[k][0][2 * p + h, t] = block[:, 48 * k : 48 * (k + 1)]

        return body

    loop(4, gv_half(0))
    va.forward(-1)
    vb.forward(-1)
    va.forward(1)
    vb.forward(1)
    vx[0].wait_recv()
    half = wvf.at[pl.ds(0, 8), pl.ds(pl.multiple_of(16 * at4(x, -1), 16), 16)]
    vxf = Group()
    send(half, half, xdev(1), vxf)
    vx[1].wait_recv()
    half = wvf.at[pl.ds(8, 8), pl.ds(pl.multiple_of(16 * at4(x, 1), 16), 16)]
    send(half, half, xdev(-1), vxf)
    loop(4, gv_half(1))
    gv.open(0)
    va.forward(2)
    vb.forward(2)
    gv.open(1)
    gv.open(2)
    vxf.wait()
    va.finish()
    vb.finish()

    for s, nr in enumerate((nrm, nrm2)):
        vals[...] = nn(nr[...], wvf[...].reshape(D, HALF_K)).astype(BF)
        mixed = (nn(lower, vals[...]) * per_count).astype(BF)
        mix_t[:, 256 * s : 256 * (s + 1)] = mixed.T
    for m in range(16):
        for u in range(2):
            mix_tb[256 * u + 16 * m : 256 * u + 16 * (m + 1), :] = mix_t[32 * m + 16 * u : 32 * m + 16 * (u + 1), :]
    go = Reduce("go", lambda p, h: p.at[:, pl.ds(256 * h, 256 - 128 * h)], lambda p: got.at[:, pl.ds(384 * p, 384)])
    for h in range(2):
        lo = HALF_D * h
        for u in range(2):
            at = slice(256 * u, 256 * (u + 1))
            g = nn(mix_tb[at, :256], cotan[:, lo : lo + HALF_D]) + nn(mix_tb[at, 256:], cot2[:, lo : lo + HALF_D])
            g = g.astype(BF).reshape(4, 4, 16, HALF_D)
            for k in range(3):
                go.bufs[k][0][2 * u + h] = g[:, :, :, 384 * k : 384 * (k + 1)]
    for p in range(3):
        go.open(p)
    for p in range(3):
        gv.turn(p)

    for s in (1, 0):

        def dn_step(g, s=s):
            w = wvf[pl.ds(8 * g, 8)].reshape(D // 2, HALF_K)
            d = nt(dval[256 * s : 256 * (s + 1), :], w)
            at = pl.ds(pl.multiple_of(g * HALF_D, 128), HALF_D)
            if s == 1:
                dn_send[:, at] = d.astype(BF)
            else:
                dn_own[:, at] = d

        loop(2, dn_step)
        if s == 1:
            dn_copy = send(dn_send, dn_recv, core)
            for p in range(3):
                gv.second(p)
            for p in range(3):
                go.turn(p)
    for p in range(3):
        gv.third(p)
    for p in range(3):
        go.second(p)
    gv.close()
    cw = send(gvw, gvw2, zdev(4))

    dn_copy.wait_recv()

    def ga_step(i):
        at = pl.ds(pl.multiple_of(i * 32, 32), 32)
        xf, inv = acts[at, :].astype(F32), inv_ref[at, :]
        scaled = gain[...].reshape(1, D) * (dn_own[at, :] + dn_recv[at, :].astype(F32))
        moment = jnp.mean(scaled * xf, axis=-1, keepdims=True)
        out = cotan[at, :].astype(F32) + inv * scaled - xf * (inv * inv * inv * moment)
        ga_out[at, :] = out.astype(BF)

    loop(8, ga_step)
    ga_copy = pltpu.make_async_copy(ga_out, ga_hbm, lsem.at[5])
    ga_copy.start()
    for p in range(3):
        go.third(p)

    cw.wait_recv()
    total = (gvw[...].astype(F32) + gvw2[...].astype(F32)).astype(BF).astype(F32)
    fin[c, x] = total
    other_rows = pl.ds(pl.multiple_of((1 - c) * 72, 8), 72)
    keep, give = fin.at[c, x, own_rows], fin.at[c, x, other_rows]
    cv = Group()
    for s in (1, -1, 2):
        send(keep, keep, xdev(s), cv)
    for s in (0, 1, -1, 2):
        send(give, give, dev(dx=s, dc=1), cv)
    go.close()
    ct = send(got, got2, zdev(4))
    cv.wait()
    pick = [picks(0), picks(1)]
    for q in range(4):
        gv_out[:, 256 * q : 256 * (q + 1)] = nn(fin[0, q, own_rows].astype(BF), pick[0]) + nn(
            fin[1, q, own_rows].astype(BF), pick[1]
        )
    ct.wait_recv()
    gof[x] = (got[...].astype(F32) + got2[...].astype(F32)).astype(BF)
    co = Group()
    for s in (1, -1, 2):
        send(gof.at[x], gof.at[x], xdev(s), co)
    ga_copy.wait()
    for k, n in enumerate(out_bytes):
        if k < len(out_bytes) - 1:
            await_bytes(n, ssem.at[k])
    co.wait()
    for u in range(2):
        for h in range(2):
            go_out[16 * u : 16 * (u + 1), HALF_D * h : HALF_D * (h + 1)] = gof[2 * u + h].astype(F32)
    await_bytes(out_bytes[-1], ssem.at[len(out_bytes) - 1])
    assert len(out_bytes) <= N_OUT and in_count[0] <= N_IN, (len(out_bytes), in_count)


def bf(*shape):
    return pltpu.VMEM(shape, BF)


def fl(*shape):
    return pltpu.VMEM(shape, F32)


INPUTS = dict(
    acts=bf(TOK, D), wv=bf(72, KVW), cotan=bf(TOK, D), cot2=bf(TOK, D), nrm=bf(TOK, D), nrm2=bf(TOK, D),
    nrmt=bf(D, 2 * TOK), inv=fl(TOK, 1), wo_a=bf(HALF_K, HALF_D), wo_b=bf(HALF_K, HALF_D),
    wvf=bf(16, 144, HALF_K), wvx=fl(144, HALF_K), wvs=fl(72, HALF_K),
)
WORK = dict(
    dmix=bf(TOK, HALF_K), dval=bf(2 * TOK, HALF_K), vals=bf(TOK, HALF_K), mix_t=bf(HALF_K, 2 * TOK),
    mix_tb=bf(HALF_K, 2 * TOK), dn_own=fl(TOK, D), dn_send=bf(TOK, D), dn_recv=bf(TOK, D), ga=bf(TOK, D),
    tally=bf(TALLY, 128),
)
LAST = dict(
    gvw=bf(144, 128), gvw2=bf(144, 128), fin=fl(2, 4, 144, 128),
    got=bf(16, HALF_D), got2=bf(16, HALF_D), gof=bf(4, 16, HALF_D),
    ssem=pltpu.SemaphoreType.DMA((N_OUT,)), rsem=pltpu.SemaphoreType.DMA((N_IN,)),
    lsem=pltpu.SemaphoreType.DMA((6,)),
)
PART = ("terms", "f0", "f1", "l1", "r1", "d1", "l2", "r2", "m2", "d2", "l3", "r3", "m3")
LEAD = ((4, 4, 4), (2, 4), (2, 4), (4, 4), (4, 4), (4, 4), (4,), (4,), (4,), (4,), (), (), ())
SCRATCH = dict(INPUTS, **WORK, **LAST)
for name, block in (("gv", (48, 128)), ("go", (16, 384))):
    for p in range(3):
        SCRATCH.update({f"{name}{p}_{n}": bf(*lead, *block) for n, lead in zip(PART, LEAD)})


def store(*refs):
    copies = [pltpu.make_async_copy(refs[k], refs[3 + k], refs[6].at[k]) for k in range(3)]
    for copy in copies:
        copy.start()
    for copy in copies:
        copy.wait()


def local(acts, value_weight, out_weight, norm_gain, cotan):
    vmem = pl.BlockSpec(memory_space=pltpu.VMEM)
    anywhere = pl.BlockSpec(memory_space=pl.ANY)
    shapes = (
        jax.ShapeDtypeStruct((72, KVW), F32),
        jax.ShapeDtypeStruct((32, D), F32),
        jax.ShapeDtypeStruct((TOK, D), BF),
    )
    outs = pl.pallas_call(
        kernel,
        out_shape=shapes,
        in_specs=[anywhere, anywhere, anywhere, vmem, anywhere],
        out_specs=(vmem, vmem, anywhere),
        scratch_shapes=list(SCRATCH.values()),
        name="fused",
        compiler_params=pltpu.CompilerParams(
            collective_id=0, has_side_effects=True, vmem_limit_bytes=60 * 2**20
        ),
    )(acts, value_weight, out_weight, norm_gain, cotan)
    return pl.pallas_call(
        store,
        out_shape=shapes,
        in_specs=[vmem] * 3,
        out_specs=(anywhere,) * 3,
        scratch_shapes=[pltpu.SemaphoreType.DMA((3,))],
        name="store",
    )(*outs)


def solution(mesh):
    placed = (
        P(("replica", "fsdp"), None),
        P("fsdp", None),
        P("fsdp", None),
        P(),
        P(("replica", "fsdp"), None),
    )
    return jax.shard_map(
        local,
        mesh=mesh,
        in_specs=placed,
        out_specs=(P("fsdp", None), P("fsdp", None), P(("replica", "fsdp"), None)),
        check_vma=False,
    )
```

```python
import math

import jax
import jax.numpy as jnp
from jax import lax
from jax.experimental import pallas as pl
from jax.experimental.pallas import tpu as pltpu
from jax.sharding import PartitionSpec as P

MESH = pl.DeviceIdType.MESH
BF, F32 = jnp.bfloat16, jnp.float32
D, KVW, TOK = 2304, 1024, 256
HALF_D, HALF_K = D // 2, KVW // 2
N_OUT, N_IN = 12, 96
TALLY = 9216


def nt(a, b):
    return lax.dot_general(a, b, (((1,), (1,)), ((), ())), preferred_element_type=F32)


def nn(a, b):
    return jnp.dot(a, b, preferred_element_type=F32)


def loop(n, body):
    def step(i, carry):
        body(i)
        return carry

    lax.fori_loop(0, n, step, 0)


def rows(ref, start, size):
    return ref.at[pl.ds(pl.multiple_of(start, 16), size)]


def kernel(*refs):
    ref = dict(zip(("acts_in", "wv_in", "wo_in", "gain", "cot_in", "gv_out", "go_out", "ga_hbm", *SCRATCH), refs))
    acts_in, wv_in, wo_in, gain, cot_in = (ref[n] for n in ("acts_in", "wv_in", "wo_in", "gain", "cot_in"))
    gv_out, go_out, ga_hbm = (ref[n] for n in ("gv_out", "go_out", "ga_hbm"))
    acts, wv, cotan, cot2, nrm, nrm2, nrmt, inv_ref, wof, wvf, wvx, wvs = (ref[n] for n in INPUTS)
    dmix, dval, vals, mix_t, mix_tb, dn_own, dn_send, dn_recv, ga_out, tally = (ref[n] for n in WORK)
    gvw, gvw2, fin, got, got2, gof, ssem, rsem, lsem = (ref[n] for n in LAST)
    r, f = lax.axis_index("replica"), lax.axis_index("fsdp")
    x, y, zl, c = r // 2, f // 8, (f // 2) % 4, f % 2
    z = (r % 2) * 4 + zl
    me = y * 4 + zl

    def dev(dx=0, dy=0, dz=0, dc=0):
        xx, yy, zz, cc = (x + dx + 4) % 4, (y + dy + 4) % 4, (z + dz + 8) % 8, (c + dc) % 2
        return (xx * 2 + zz // 4, yy * 8 + (zz % 4) * 2 + cc)

    def ydev(s):
        return dev(dy=s)

    def zdev(s):
        return dev(dz=s)

    def xdev(s):
        return dev(dx=s)

    def at4(q, s):
        return (q + s + 4) % 4

    own_unit = pl.ds(pl.multiple_of(128 * x, 128), 128)
    own_wo = [
        pltpu.make_async_copy(wo_in.at[:, cols], wof.at[me, :, cols], lsem.at[h])
        for h, cols in enumerate((own_unit, pl.ds(512, D - 512)))
    ]
    own_wv = pltpu.make_async_copy(wv_in, wv, lsem.at[2])
    own_cot = pltpu.make_async_copy(cot_in, cotan, lsem.at[3])
    own_acts = pltpu.make_async_copy(acts_in, acts, lsem.at[4])
    for copy in (*own_wo, own_wv, own_cot, own_acts):
        copy.start()

    core = dev(dc=1)
    partners = [core, *(xdev(s) for s in (1, -1, 2)), *(dev(dx=s, dc=1) for s in (1, -1, 2))]
    partners += [*(ydev(s) for s in (1, -1, 2)), *(zdev(s) for s in (1, -1, 2, -2, 4))]
    barrier = pltpu.get_barrier_semaphore()
    for p in partners:
        pl.semaphore_signal(barrier, inc=1, device_id=p, device_id_type=MESH)
    pl.semaphore_wait(barrier, len(partners))

    def await_bytes(n, sem):
        view = tally.at[pl.ds(0, n // 256)]
        pltpu.make_async_copy(view, view, sem).wait()

    out_bytes, in_count = [0], [0]

    class Group:
        def __init__(self):
            self.i, self.bytes = in_count[0], 0
            in_count[0] += 1

        def wait(self):
            await_bytes(self.bytes, rsem.at[self.i])

    def send(src, dst, to, group=None):
        n = math.prod(src.shape) * jnp.dtype(src.dtype).itemsize
        if out_bytes[-1] + n > TALLY * 256:
            out_bytes.append(0)
        out_bytes[-1] += n
        alone = group is None
        group = Group() if alone else group
        group.bytes += n
        copy = pltpu.make_async_remote_copy(
            src_ref=src, dst_ref=dst, send_sem=ssem.at[len(out_bytes) - 1], recv_sem=rsem.at[group.i],
            device_id=to, device_id_type=MESH,
        )
        copy.start()
        return copy if alone else None

    class Gather:
        def __init__(self, first, second, block):
            self.first, self.second, self.block = first, second, block
            self.p2, self.rest = {}, Group()

        def spread(self, to, block, near, far):
            b = block(None)
            copies = (send(b, b, to(1), near), send(b, b, to(-1), near))
            if to is zdev:
                h0, h1 = block(0), block(1)
                send(h0, h0, to(2), far)
                send(h1, h1, to(-2), far)
            else:
                send(b, b, to(2), far)
            return copies

        def own(self):
            self.p1far = Group()
            self.p1 = self.spread(self.first, lambda h: self.block(0, 0, h), None, self.p1far)

        def chunk(self, i):
            b = self.block(i, 0, None)
            self.p2[i] = (send(b, b, self.second(1)), send(b, b, self.second(-1)))

        def direct(self, i):
            self.spread(self.second, lambda h: self.block(i, 0, h), self.rest, self.rest)

        def near(self, then):
            self.p1[0].wait_recv()
            then(-1)
            self.p1[1].wait_recv()
            then(1)

        def far(self, then):
            self.p1far.wait()
            then(2)

        def forward(self, i):
            up, down = self.p2[i]
            up.wait_recv()
            b = self.block(i, -1, 0)
            send(b, b, self.second(1), self.rest)
            down.wait_recv()
            b = self.block(i, 1, 1)
            send(b, b, self.second(-1), self.rest)

        def finish(self):
            self.rest.wait()

    def slot_yz(i, j):
        return at4(y, i) * 4 + at4(zl, j)

    def slot_zy(i, j):
        return at4(y, j) * 4 + at4(zl, i)

    def wo_block(slot, lo, n):
        def block(i, j, half):
            at = wof.at[slot(i, j), :, pl.ds(lo, n)]
            return at if half is None else at.at[pl.ds(16 * half, 16)]

        return block

    def wo_shared(i, j, half):
        at = wof.at[slot_yz(i, j), :, own_unit]
        return at if half is None else at.at[pl.ds(16 * half, 16)]

    def wv_block(slot, lo, n):
        def block(i, j, half):
            at = wvf.at[slot(i, j), pl.ds(lo, n)]
            return at if half is None else at.at[:, pl.ds(256 * half, 256)]

        return block

    def wv_shared(i, j, half):
        at = wvf.at[slot_zy(i, j), pl.ds(pl.multiple_of(16 * x, 16), 16)]
        return at if half is None else at.at[:, pl.ds(256 * half, 256)]

    class Sum:
        def __init__(self, own, left, right, far):
            self.own, self.left, self.right, self.far = own, left, right, far
            self.group = Group()

        def close(self, out):
            self.group.wait()
            total = self.own[...].astype(F32) + self.left[...].astype(F32)
            total += self.right[...].astype(F32) + self.far[...].astype(F32)
            out[...] = total.astype(BF)

    def direct(to, part, left, right, far, halves):
        got_sum = Sum(part(0), left, right, far)
        send(part(1), left, to(1), got_sum.group)
        send(part(-1), right, to(-1), got_sum.group)
        p = part(2)
        if to is zdev:
            for h, hop in enumerate((2, -2)):
                send(halves(p, h), halves(far, h), to(hop), got_sum.group)
        else:
            send(p, far, to(2), got_sum.group)
        return got_sum

    def two(p, h):
        return p.at[pl.ds(2 * h, 2)]

    class Ring:
        def __init__(self, to, part, f0, f1, left, right):
            self.to, self.part = to, part
            self.f0, self.f1, self.left, self.right = f0, f1, left, right

        def recv(self, ref, h):
            return ref.at[pl.ds(2 * h, 2)]

        def open(self):
            self.rest = Group()
            self.c0 = send(self.part(2, 0), self.f0, self.to(1))
            self.c1 = send(self.part(2, 1), self.f1, self.to(-1))
            send(self.part(1, 1), self.recv(self.left, 1), self.to(1), self.rest)
            send(self.part(-1, 0), self.recv(self.right, 0), self.to(-1), self.rest)

        def turn(self):
            self.c0.wait_recv()
            h = self.part(1, 0)
            h[...] = (h[...].astype(F32) + self.f0[...].astype(F32)).astype(BF)
            send(h, self.recv(self.left, 0), self.to(1), self.rest)
            self.c1.wait_recv()
            h = self.part(-1, 1)
            h[...] = (h[...].astype(F32) + self.f1[...].astype(F32)).astype(BF)
            send(h, self.recv(self.right, 1), self.to(-1), self.rest)

        def close(self, out):
            self.rest.wait()
            for h in range(2):
                total = self.part(0, h)[...].astype(F32) + self.recv(self.left, h)[...].astype(F32)
                total += self.recv(self.right, h)[...].astype(F32)
                o = self.recv(out, h)
                o[...] = total.astype(BF)

    class Reduce:
        def __init__(self, name, halves):
            self.bufs = [[ref[f"{name}{p}_{n}"] for n in PART] for p in range(3)]
            self.halves = halves
            bx, by, bz = (b[0] for b in self.bufs)
            own = (bx.at[x], by.at[:, y], bz.at[:, :, zl])
            self.sums = [Sum(own[p], *self.bufs[p][1:4]) if name == "go" else None for p in range(3)]

        def open_rings(self):
            bx, by, bz = (b[0] for b in self.bufs)
            parts = (
                (xdev, lambda s, h: bx.at[at4(x, s), pl.ds(2 * h, 2)]),
                (ydev, lambda s, h: by.at[pl.ds(2 * h, 2), at4(y, s)]),
                (zdev, lambda s, h: bz.at[pl.ds(2 * h, 2), :, at4(zl, s)]),
            )
            for p in range(3):
                self.sums[p] = Ring(*parts[p], ref[f"gv{p}_f0"], ref[f"gv{p}_f1"], *self.bufs[p][1:3])
                self.sums[p].open()

        def open_x(self, s):
            land = {1: 1, -1: 2, 2: 3}[s]
            send(self.bufs[0][0].at[at4(x, s)], self.bufs[0][land], xdev(s), self.sums[0].group)

        def open_yz(self, units):
            by, lefty, righty, fary = self.bufs[1][:4]
            bz, leftz, rightz, farz = self.bufs[2][:4]
            for s, land in ((2, fary), (1, lefty), (-1, righty)):
                send(by.at[units, at4(y, s)], land.at[units], ydev(s), self.sums[1].group)
            for h, hop in enumerate((2, -2)):
                at = pl.ds(2 * h, 2)
                send(bz.at[units, at, at4(zl, 2)], farz.at[units, at], zdev(hop), self.sums[2].group)
            for s, land in ((1, leftz), (-1, rightz)):
                send(bz.at[units, :, at4(zl, s)], land.at[units], zdev(s), self.sums[2].group)

        def second(self, p):
            done = self.bufs[p][4]
            self.sums[p].close(done)
            to, part = (
                (ydev, lambda s: done.at[at4(y, s)]),
                (zdev, lambda s: done.at[:, at4(zl, s)]),
                (xdev, lambda s: done.at[at4(x, s)]),
            )[p]
            self.sums[p] = direct(to, part, *self.bufs[p][5:8], two)

        def third(self, p):
            done = self.bufs[p][8]
            self.sums[p].close(done)
            to, q = ((zdev, zl), (xdev, x), (ydev, y))[p]
            self.sums[p] = direct(to, lambda s: done.at[at4(q, s)], *self.bufs[p][9:12], self.halves)

    gv = Reduce("gv", lambda p, h: p.at[pl.ds(32 * h, 32 - 16 * h)])
    go = Reduce("go", lambda p, h: p.at[:, pl.ds(256 * h, 256 - 128 * h)])

    class Share:
        def __init__(self, pick):
            self.pick, self.rest = pick, Group()
            p = pick(0, pl.ds(0, 16))
            self.up, self.down = send(p, p, xdev(1)), send(p, p, xdev(-1))

        def forward(self):
            self.up.wait_recv()
            p = self.pick(-1, pl.ds(0, 8))
            send(p, p, xdev(1), self.rest)
            self.down.wait_recv()
            p = self.pick(1, pl.ds(8, 8))
            send(p, p, xdev(-1), self.rest)

    def wo_units(s, blocks):
        return wof.at[blocks, :, pl.ds(pl.multiple_of(128 * at4(x, s), 128), 128)]

    def wv_units(s, blocks):
        return wvf.at[blocks, pl.ds(pl.multiple_of(16 * at4(x, s), 16), 16)]

    gs = Gather(ydev, zdev, wo_shared)
    ga = Gather(ydev, zdev, wo_block(slot_yz, 512, 896))
    gb = Gather(zdev, ydev, wo_block(slot_zy, 1408, 896))
    for copy in own_wo:
        copy.wait()
    gs.own()
    gs.direct(0)
    ga.own()
    gb.own()
    ga.chunk(0)
    gb.chunk(0)

    jj = lax.broadcasted_iota(jnp.int32, (128, 256), 0)
    kk = lax.broadcasted_iota(jnp.int32, (128, 256), 1)
    base = 64 * (jj // 32) + jj % 32

    def picks(which):
        return (kk == base + 32 * which).astype(BF)

    pick_own, pick_other = picks(c), picks(1 - c)
    own_rows = pl.ds(pl.multiple_of(c * 72, 8), 72)
    own_wv.wait()
    for q in range(4):
        group = wv[:, 256 * q : 256 * (q + 1)]
        wvs[:, 128 * q : 128 * (q + 1)] = nt(group, pick_other)
    wvx_copy = send(wvs, wvx.at[own_rows], core)
    for q in range(4):
        group = wv[:, 256 * q : 256 * (q + 1)]
        wvx[own_rows, 128 * q : 128 * (q + 1)] = nt(group, pick_own)
    own_cot.wait()
    cot_copy = send(cotan, cot2, core)

    own_acts.wait()

    def norm_step(i):
        at = pl.ds(pl.multiple_of(i * 32, 32), 32)
        xf = acts[at, :].astype(F32)
        inv = lax.rsqrt(jnp.mean(xf * xf, axis=-1, keepdims=True) + 1e-06)
        inv_ref[at, :] = inv
        nrm[at, :] = (xf * inv * gain[...].reshape(1, D)).astype(BF)

    loop(8, norm_step)
    nrm_copy = send(nrm, nrm2, core)

    wvx_copy.wait_recv()
    mine = pl.ds(pl.multiple_of(16 * x, 16), 16)
    wvf[me, mine] = wvx[mine, :].astype(BF)
    wvf[me, 64:144] = wvx[64:144].astype(BF)
    vs = Gather(zdev, ydev, wv_shared)
    vs.own()
    vs.direct(0)
    gs.near(gs.direct)
    gs.far(gs.direct)
    ga.near(ga.chunk)
    gb.near(gb.chunk)
    ga.far(ga.chunk)
    gb.far(gb.chunk)
    vs.near(vs.direct)
    vs.far(vs.direct)
    ga.forward(0)
    gb.forward(0)
    gs.finish()
    wo_share = Share(wo_units)
    ga.forward(-1)
    gb.forward(-1)
    ga.forward(1)
    gb.forward(1)
    va = Gather(ydev, zdev, wv_block(slot_yz, 64, 48))
    vb = Gather(zdev, ydev, wv_block(slot_zy, 112, 32))

    def turn_step(src, at):
        def body(t):
            lanes = pl.ds(pl.multiple_of(t * 256, 256), 256)
            nrmt[lanes, at * 256 : (at + 1) * 256] = src[:, lanes].T

        return body

    loop(9, turn_step(nrm, 0))
    ga.forward(2)
    gb.forward(2)
    va.own()
    vb.own()
    va.chunk(0)
    vb.chunk(0)
    wo_share.forward()
    vs.finish()
    wv_share = Share(wv_units)
    nrm_copy.wait_recv()
    loop(9, turn_step(nrm2, 1))
    va.near(va.chunk)
    vb.near(vb.chunk)
    va.far(va.chunk)
    vb.far(vb.chunk)
    cot_copy.wait_recv()
    ga.finish()
    gb.finish()
    wo_share.rest.wait()

    ri = lax.broadcasted_iota(jnp.int32, (TOK, TOK), 0)
    ci = lax.broadcasted_iota(jnp.int32, (TOK, TOK), 1)
    lower = (ri >= ci).astype(BF)
    upper = (ci >= ri).astype(BF)
    per_count = 1.0 / (lax.broadcasted_iota(jnp.int32, (TOK, 1), 0) + 1).astype(F32)

    for s, cot in enumerate((cotan, cot2)):

        def dmix_step(n, cot=cot, s=s):
            at = pl.ds(pl.multiple_of(n * 256, 256), 256)
            d = nt(cot[...], wof[pl.ds(8 * n, 8)].reshape(256, D))
            dmix[:, at] = (d * per_count).astype(BF)

        loop(2, dmix_step)
        dval[256 * s : 256 * (s + 1), :] = nn(upper, dmix[...]).astype(BF)
        va.forward((0, -1)[s])
        vb.forward((0, -1)[s])

    def gv_half(p):
        def body(t):
            at = pl.ds(pl.multiple_of(t * 576, 16), 576)
            g = nn(nrmt[at, :], dval[:, 256 * p : 256 * (p + 1)]).astype(BF)
            for h in range(2):
                block = g[:, 128 * h : 128 * (h + 1)].reshape(4, 144, 128)
                for k in range(3):
                    gv.bufs[k][0][2 * p + h, t] = block[:, 48 * k : 48 * (k + 1)]

        return body

    loop(4, gv_half(0))
    va.forward(1)
    vb.forward(1)
    wv_share.forward()
    va.forward(2)
    vb.forward(2)
    loop(4, gv_half(1))
    gv.open_rings()
    va.finish()
    vb.finish()
    wv_share.rest.wait()

    for s, nr in enumerate((nrm, nrm2)):
        vals[...] = nn(nr[...], wvf[...].reshape(D, HALF_K)).astype(BF)
        mixed = (nn(lower, vals[...]) * per_count).astype(BF)
        mix_t[:, 256 * s : 256 * (s + 1)] = mixed.T
    for m in range(16):
        for u in range(2):
            mix_tb[256 * u + 16 * m : 256 * u + 16 * (m + 1), :] = mix_t[32 * m + 16 * u : 32 * m + 16 * (u + 1), :]
    for s in (2, 1, -1, 0):
        d = at4(x, s)
        at = pl.ds(pl.multiple_of(256 * (d // 2), 256), 256)
        lanes = pl.ds(pl.multiple_of(HALF_D * (d % 2), 128), HALF_D)
        g = nn(mix_tb[at, :256], cotan[:, lanes]) + nn(mix_tb[at, 256:], cot2[:, lanes])
        g = g.astype(BF).reshape(4, 4, 16, HALF_D)
        for k in range(3):
            go.bufs[k][0][d] = g[:, :, :, 384 * k : 384 * (k + 1)]
        if s != 0:
            go.open_x(s)
        go.open_yz(pl.ds(d, 1))

    for p in range(3):
        gv.sums[p].turn()

    for s in (1, 0):

        def dn_step(g, s=s):
            w = wvf[pl.ds(8 * g, 8)].reshape(D // 2, HALF_K)
            d = nt(dval[256 * s : 256 * (s + 1), :], w)
            at = pl.ds(pl.multiple_of(g * HALF_D, 128), HALF_D)
            if s == 1:
                dn_send[:, at] = d.astype(BF)
            else:
                dn_own[:, at] = d

        loop(2, dn_step)
        if s == 1:
            dn_copy = send(dn_send, dn_recv, core)
    for p in range(3):
        gv.second(p)

    dn_copy.wait_recv()

    def ga_step(i):
        at = pl.ds(pl.multiple_of(i * 32, 32), 32)
        xf, inv = acts[at, :].astype(F32), inv_ref[at, :]
        scaled = gain[...].reshape(1, D) * (dn_own[at, :] + dn_recv[at, :].astype(F32))
        moment = jnp.mean(scaled * xf, axis=-1, keepdims=True)
        out = cotan[at, :].astype(F32) + inv * scaled - xf * (inv * inv * inv * moment)
        ga_out[at, :] = out.astype(BF)

    loop(8, ga_step)
    ga_copy = pltpu.make_async_copy(ga_out, ga_hbm, lsem.at[5])
    ga_copy.start()
    for p in range(3):
        go.second(p)
    for p in range(3):
        gv.third(p)

    for p in range(3):
        go.third(p)
    cw, ct = Group(), Group()
    for p in range(3):
        part, land = gvw.at[pl.ds(48 * p, 48)], gvw2.at[pl.ds(48 * p, 48)]
        gv.sums[p].close(part)
        send(part, land, zdev(4), cw)
    for p in range(3):
        part, land = got.at[:, pl.ds(384 * p, 384)], got2.at[:, pl.ds(384 * p, 384)]
        go.sums[p].close(part)
        send(part, land, zdev(4), ct)
    cw.wait()
    total = gvw[...].astype(F32) + gvw2[...].astype(F32)
    for h in range(2):
        fin[h, c, x, 0:72] = total[72 * h : 72 * (h + 1)].astype(BF)
    keep, give = fin.at[c, c, x], fin.at[1 - c, c, x]
    cv = Group()
    for s in (1, -1, 2):
        send(keep, keep, xdev(s), cv)
    for s in (0, 1, -1, 2):
        send(give, give, dev(dx=s, dc=1), cv)
    ct.wait()
    gof[x] = (got[...].astype(F32) + got2[...].astype(F32)).astype(BF)
    co = Group()
    for s in (1, -1, 2):
        send(gof.at[x], gof.at[x], xdev(s), co)
    cv.wait()
    pick = [picks(0), picks(1)]
    for q in range(4):
        g = nn(fin[c, 0, q], pick[0]) + nn(fin[c, 1, q], pick[1])
        gv_out[:, 256 * q : 256 * (q + 1)] = g[0:72]
    ga_copy.wait()
    for k, n in enumerate(out_bytes):
        if k < len(out_bytes) - 1:
            await_bytes(n, ssem.at[k])
    co.wait()
    for u in range(2):
        for h in range(2):
            go_out[16 * u : 16 * (u + 1), HALF_D * h : HALF_D * (h + 1)] = gof[2 * u + h].astype(F32)
    await_bytes(out_bytes[-1], ssem.at[len(out_bytes) - 1])
    assert len(out_bytes) <= N_OUT and in_count[0] <= N_IN, (len(out_bytes), in_count)


def bf(*shape):
    return pltpu.VMEM(shape, BF)


def fl(*shape):
    return pltpu.VMEM(shape, F32)


INPUTS = dict(
    acts=bf(TOK, D), wv=bf(72, KVW), cotan=bf(TOK, D), cot2=bf(TOK, D), nrm=bf(TOK, D), nrm2=bf(TOK, D),
    nrmt=bf(D, 2 * TOK), inv=fl(TOK, 1), wof=bf(16, 32, D),
    wvf=bf(16, 144, HALF_K), wvx=fl(144, HALF_K), wvs=fl(72, HALF_K),
)
WORK = dict(
    dmix=bf(TOK, HALF_K), dval=bf(2 * TOK, HALF_K), vals=bf(TOK, HALF_K), mix_t=bf(HALF_K, 2 * TOK),
    mix_tb=bf(HALF_K, 2 * TOK), dn_own=fl(TOK, D), dn_send=bf(TOK, D), dn_recv=bf(TOK, D), ga=bf(TOK, D),
    tally=bf(TALLY, 128),
)
LAST = dict(
    gvw=bf(144, 128), gvw2=bf(144, 128), fin=bf(2, 2, 4, 80, 128),
    got=bf(16, HALF_D), got2=bf(16, HALF_D), gof=bf(4, 16, HALF_D),
    ssem=pltpu.SemaphoreType.DMA((N_OUT,)), rsem=pltpu.SemaphoreType.DMA((N_IN,)),
    lsem=pltpu.SemaphoreType.DMA((6,)),
)
PART = ("terms", "l1", "r1", "m1", "d1", "l2", "r2", "m2", "d2", "l3", "r3", "m3")
LEAD = ((4, 4, 4), (4, 4), (4, 4), (4, 4), (4, 4), (4,), (4,), (4,), (4,), (), (), ())
SCRATCH = dict(INPUTS, **WORK, **LAST)
for name, block in (("gv", (48, 128)), ("go", (16, 384))):
    for p in range(3):
        SCRATCH.update({f"{name}{p}_{n}": bf(*lead, *block) for n, lead in zip(PART, LEAD)})
        if name == "gv":
            SCRATCH.update({f"gv{p}_f{h}": bf(2, 4, *block) for h in range(2)})


def store(*refs):
    copies = [pltpu.make_async_copy(refs[k], refs[3 + k], refs[6].at[k]) for k in range(3)]
    for copy in copies:
        copy.start()
    for copy in copies:
        copy.wait()


def local(acts, value_weight, out_weight, norm_gain, cotan):
    vmem = pl.BlockSpec(memory_space=pltpu.VMEM)
    anywhere = pl.BlockSpec(memory_space=pl.ANY)
    shapes = (
        jax.ShapeDtypeStruct((72, KVW), F32),
        jax.ShapeDtypeStruct((32, D), F32),
        jax.ShapeDtypeStruct((TOK, D), BF),
    )
    outs = pl.pallas_call(
        kernel,
        out_shape=shapes,
        in_specs=[anywhere, anywhere, anywhere, vmem, anywhere],
        out_specs=(vmem, vmem, anywhere),
        scratch_shapes=list(SCRATCH.values()),
        name="fused",
        compiler_params=pltpu.CompilerParams(
            collective_id=0, has_side_effects=True, vmem_limit_bytes=60 * 2**20
        ),
    )(acts, value_weight, out_weight, norm_gain, cotan)
    return pl.pallas_call(
        store,
        out_shape=shapes,
        in_specs=[vmem] * 3,
        out_specs=(anywhere,) * 3,
        scratch_shapes=[pltpu.SemaphoreType.DMA((3,))],
        name="store",
    )(*outs)


def solution(mesh):
    placed = (
        P(("replica", "fsdp"), None),
        P("fsdp", None),
        P("fsdp", None),
        P(),
        P(("replica", "fsdp"), None),
    )
    return jax.shard_map(
        local,
        mesh=mesh,
        in_specs=placed,
        out_specs=(P("fsdp", None), P("fsdp", None), P(("replica", "fsdp"), None)),
        check_vma=False,
    )
```

```python
import math

import jax
import jax.numpy as jnp
from jax import lax
from jax.experimental import pallas as pl
from jax.experimental.pallas import tpu as pltpu
from jax.sharding import PartitionSpec as P

MESH = pl.DeviceIdType.MESH
BF, F32 = jnp.bfloat16, jnp.float32
D, KVW, TOK = 2304, 1024, 256
HALF_D, HALF_K = D // 2, KVW // 2
N_OUT, N_IN = 12, 96
TALLY = 9216


def nt(a, b):
    return lax.dot_general(a, b, (((1,), (1,)), ((), ())), preferred_element_type=F32)


def nn(a, b):
    return jnp.dot(a, b, preferred_element_type=F32)


def loop(n, body):
    def step(i, carry):
        body(i)
        return carry

    lax.fori_loop(0, n, step, 0)


def rows(ref, start, size):
    return ref.at[pl.ds(pl.multiple_of(start, 16), size)]


def kernel(*refs):
    ref = dict(zip(("acts_in", "wv_in", "wo_in", "gain_in", "cot_in", "gv_out", "go_out", "ga_out", *SCRATCH), refs))
    acts_in, wv_in, wo_in, gain_in, cot_in = (ref[n] for n in ("acts_in", "wv_in", "wo_in", "gain_in", "cot_in"))
    gv_out, go_out, ga_out = (ref[n] for n in ("gv_out", "go_out", "ga_out"))
    acts, wv, cotan, gain, cot2, nrm, nrm2, nrmt, inv_ref, wof, wvf, wvx, wvs = (ref[n] for n in INPUTS)
    dmix, dval, vals, mix_t, mix_tb, dn_own, dn_send, dn_recv, tally = (ref[n] for n in WORK)
    gvw, gvw2, fin, got, got2, gof, ssem, rsem, lsem = (ref[n] for n in LAST)
    r, f = lax.axis_index("replica"), lax.axis_index("fsdp")
    x, y, zl, c = r // 2, f // 8, (f // 2) % 4, f % 2
    z = (r % 2) * 4 + zl
    me = y * 4 + zl

    def dev(dx=0, dy=0, dz=0, dc=0):
        xx, yy, zz, cc = (x + dx + 4) % 4, (y + dy + 4) % 4, (z + dz + 8) % 8, (c + dc) % 2
        return (xx * 2 + zz // 4, yy * 8 + (zz % 4) * 2 + cc)

    def ydev(s):
        return dev(dy=s)

    def zdev(s):
        return dev(dz=s)

    def xdev(s):
        return dev(dx=s)

    def at4(q, s):
        return (q + s + 4) % 4

    own_unit = pl.ds(pl.multiple_of(128 * x, 128), 128)
    own_wo = [
        pltpu.make_async_copy(wo_in.at[:, cols], wof.at[me, :, cols], lsem.at[h])
        for h, cols in enumerate((own_unit, pl.ds(512, D - 512)))
    ]
    own_wv = pltpu.make_async_copy(wv_in, wv, lsem.at[2])
    own_cot = pltpu.make_async_copy(cot_in, cotan, lsem.at[3])
    own_acts = pltpu.make_async_copy(acts_in, acts, lsem.at[4])
    own_gain = pltpu.make_async_copy(gain_in, gain, lsem.at[5])
    for copy in (*own_wo, own_wv, own_cot, own_acts, own_gain):
        copy.start()

    core = dev(dc=1)
    partners = [core, *(xdev(s) for s in (1, -1, 2)), *(dev(dx=s, dc=1) for s in (1, -1, 2))]
    partners += [*(ydev(s) for s in (1, -1, 2)), *(zdev(s) for s in (1, -1, 2, -2, 4))]
    barrier = pltpu.get_barrier_semaphore()
    for p in partners:
        pl.semaphore_signal(barrier, inc=1, device_id=p, device_id_type=MESH)
    pl.semaphore_wait(barrier, len(partners))

    def await_bytes(n, sem):
        view = tally.at[pl.ds(0, n // 256)]
        pltpu.make_async_copy(view, view, sem).wait()

    out_bytes, in_count = [0], [0]

    class Group:
        def __init__(self):
            self.i, self.bytes = in_count[0], 0
            in_count[0] += 1

        def wait(self):
            await_bytes(self.bytes, rsem.at[self.i])

    def send(src, dst, to, group=None):
        n = math.prod(src.shape) * jnp.dtype(src.dtype).itemsize
        if out_bytes[-1] + n > TALLY * 256:
            out_bytes.append(0)
        out_bytes[-1] += n
        alone = group is None
        group = Group() if alone else group
        group.bytes += n
        copy = pltpu.make_async_remote_copy(
            src_ref=src, dst_ref=dst, send_sem=ssem.at[len(out_bytes) - 1], recv_sem=rsem.at[group.i],
            device_id=to, device_id_type=MESH,
        )
        copy.start()
        return copy if alone else None

    class Gather:
        def __init__(self, first, second, block):
            self.first, self.second, self.block = first, second, block
            self.p2, self.rest = {}, Group()

        def spread(self, to, block, near, far):
            b = block(None)
            copies = (send(b, b, to(1), near), send(b, b, to(-1), near))
            if to is zdev:
                h0, h1 = block(0), block(1)
                send(h0, h0, to(2), far)
                send(h1, h1, to(-2), far)
            else:
                send(b, b, to(2), far)
            return copies

        def own(self):
            self.p1far = Group()
            self.p1 = self.spread(self.first, lambda h: self.block(0, 0, h), None, self.p1far)

        def chunk(self, i):
            b = self.block(i, 0, None)
            self.p2[i] = (send(b, b, self.second(1)), send(b, b, self.second(-1)))

        def direct(self, i):
            self.spread(self.second, lambda h: self.block(i, 0, h), self.rest, self.rest)

        def near(self, then):
            self.p1[0].wait_recv()
            then(-1)
            self.p1[1].wait_recv()
            then(1)

        def far(self, then):
            self.p1far.wait()
            then(2)

        def forward(self, i):
            up, down = self.p2[i]
            up.wait_recv()
            b = self.block(i, -1, 0)
            send(b, b, self.second(1), self.rest)
            down.wait_recv()
            b = self.block(i, 1, 1)
            send(b, b, self.second(-1), self.rest)

        def finish(self):
            self.rest.wait()

    def slot_yz(i, j):
        return at4(y, i) * 4 + at4(zl, j)

    def slot_zy(i, j):
        return at4(y, j) * 4 + at4(zl, i)

    def wo_block(slot, lo, n):
        def block(i, j, half):
            at = wof.at[slot(i, j), :, pl.ds(lo, n)]
            return at if half is None else at.at[pl.ds(16 * half, 16)]

        return block

    def wo_shared(i, j, half):
        at = wof.at[slot_yz(i, j), :, own_unit]
        return at if half is None else at.at[pl.ds(16 * half, 16)]

    def wv_block(slot, lo, n):
        def block(i, j, half):
            at = wvf.at[slot(i, j), pl.ds(lo, n)]
            return at if half is None else at.at[:, pl.ds(256 * half, 256)]

        return block

    def wv_shared(i, j, half):
        at = wvf.at[slot_zy(i, j), pl.ds(pl.multiple_of(16 * x, 16), 16)]
        return at if half is None else at.at[:, pl.ds(256 * half, 256)]

    class Sum:
        def __init__(self, own, left, right, far):
            self.own, self.left, self.right, self.far = own, left, right, far
            self.group = Group()

        def close(self, out):
            self.group.wait()
            total = self.own[...].astype(F32) + self.left[...].astype(F32)
            total += self.right[...].astype(F32) + self.far[...].astype(F32)
            out[...] = total.astype(BF)

    def direct(to, part, left, right, far, halves):
        got_sum = Sum(part(0), left, right, far)
        send(part(1), left, to(1), got_sum.group)
        send(part(-1), right, to(-1), got_sum.group)
        p = part(2)
        if to is zdev:
            for h, hop in enumerate((2, -2)):
                send(halves(p, h), halves(far, h), to(hop), got_sum.group)
        else:
            send(p, far, to(2), got_sum.group)
        return got_sum

    def two(p, h):
        return p.at[pl.ds(2 * h, 2)]

    class Ring:
        def __init__(self, to, part, f0, f1, left, right):
            self.to, self.part = to, part
            self.f0, self.f1, self.left, self.right = f0, f1, left, right

        def recv(self, ref, h):
            return ref.at[pl.ds(2 * h, 2)]

        def open(self):
            self.rest = Group()
            self.c0 = send(self.part(2, 0), self.f0, self.to(1))
            self.c1 = send(self.part(2, 1), self.f1, self.to(-1))
            send(self.part(1, 1), self.recv(self.left, 1), self.to(1), self.rest)
            send(self.part(-1, 0), self.recv(self.right, 0), self.to(-1), self.rest)

        def turn(self):
            self.c0.wait_recv()
            h = self.part(1, 0)
            h[...] = (h[...].astype(F32) + self.f0[...].astype(F32)).astype(BF)
            send(h, self.recv(self.left, 0), self.to(1), self.rest)
            self.c1.wait_recv()
            h = self.part(-1, 1)
            h[...] = (h[...].astype(F32) + self.f1[...].astype(F32)).astype(BF)
            send(h, self.recv(self.right, 1), self.to(-1), self.rest)

        def close(self, out):
            self.rest.wait()
            for h in range(2):
                total = self.part(0, h)[...].astype(F32) + self.recv(self.left, h)[...].astype(F32)
                total += self.recv(self.right, h)[...].astype(F32)
                o = self.recv(out, h)
                o[...] = total.astype(BF)

    class Reduce:
        def __init__(self, name, halves):
            self.bufs = [[ref[f"{name}{p}_{n}"] for n in PART] for p in range(3)]
            self.halves = halves
            bx, by, bz = (b[0] for b in self.bufs)
            own = (bx.at[x], by.at[:, y], bz.at[:, :, zl])
            self.sums = [Sum(own[p], *self.bufs[p][1:4]) if name == "go" else None for p in range(3)]

        def open_rings(self):
            bx, by, bz = (b[0] for b in self.bufs)
            parts = (
                (xdev, lambda s, h: bx.at[at4(x, s), pl.ds(2 * h, 2)]),
                (ydev, lambda s, h: by.at[pl.ds(2 * h, 2), at4(y, s)]),
                (zdev, lambda s, h: bz.at[pl.ds(2 * h, 2), :, at4(zl, s)]),
            )
            for p in range(3):
                self.sums[p] = Ring(*parts[p], ref[f"gv{p}_f0"], ref[f"gv{p}_f1"], *self.bufs[p][1:3])
                self.sums[p].open()

        def open_x(self, s):
            land = {1: 1, -1: 2, 2: 3}[s]
            send(self.bufs[0][0].at[at4(x, s)], self.bufs[0][land], xdev(s), self.sums[0].group)

        def open_yz(self, units):
            by, lefty, righty, fary = self.bufs[1][:4]
            bz, leftz, rightz, farz = self.bufs[2][:4]
            for s, land in ((2, fary), (1, lefty), (-1, righty)):
                send(by.at[units, at4(y, s)], land.at[units], ydev(s), self.sums[1].group)
            for h, hop in enumerate((2, -2)):
                at = pl.ds(2 * h, 2)
                send(bz.at[units, at, at4(zl, 2)], farz.at[units, at], zdev(hop), self.sums[2].group)
            for s, land in ((1, leftz), (-1, rightz)):
                send(bz.at[units, :, at4(zl, s)], land.at[units], zdev(s), self.sums[2].group)

        def second(self, p):
            done = self.bufs[p][4]
            self.sums[p].close(done)
            to, part = (
                (ydev, lambda s: done.at[at4(y, s)]),
                (zdev, lambda s: done.at[:, at4(zl, s)]),
                (xdev, lambda s: done.at[at4(x, s)]),
            )[p]
            self.sums[p] = direct(to, part, *self.bufs[p][5:8], two)

        def third(self, p):
            done = self.bufs[p][8]
            self.sums[p].close(done)
            to, q = ((zdev, zl), (xdev, x), (ydev, y))[p]
            self.sums[p] = direct(to, lambda s: done.at[at4(q, s)], *self.bufs[p][9:12], self.halves)

    gv = Reduce("gv", lambda p, h: p.at[pl.ds(32 * h, 32 - 16 * h)])
    go = Reduce("go", lambda p, h: p.at[:, pl.ds(256 * h, 256 - 128 * h)])

    class Share:
        def __init__(self, pick):
            self.pick, self.rest = pick, Group()
            p = pick(0, pl.ds(0, 16))
            self.up, self.down = send(p, p, xdev(1)), send(p, p, xdev(-1))

        def forward(self):
            self.up.wait_recv()
            p = self.pick(-1, pl.ds(0, 8))
            send(p, p, xdev(1), self.rest)
            self.down.wait_recv()
            p = self.pick(1, pl.ds(8, 8))
            send(p, p, xdev(-1), self.rest)

    def wo_units(s, blocks):
        return wof.at[blocks, :, pl.ds(pl.multiple_of(128 * at4(x, s), 128), 128)]

    def wv_units(s, blocks):
        return wvf.at[blocks, pl.ds(pl.multiple_of(16 * at4(x, s), 16), 16)]

    gs = Gather(ydev, zdev, wo_shared)
    ga = Gather(ydev, zdev, wo_block(slot_yz, 512, 896))
    gb = Gather(zdev, ydev, wo_block(slot_zy, 1408, 896))
    for copy in own_wo:
        copy.wait()
    gs.own()
    gs.direct(0)
    ga.own()
    gb.own()
    ga.chunk(0)
    gb.chunk(0)

    jj = lax.broadcasted_iota(jnp.int32, (128, 256), 0)
    kk = lax.broadcasted_iota(jnp.int32, (128, 256), 1)
    base = 64 * (jj // 32) + jj % 32

    def picks(which):
        return (kk == base + 32 * which).astype(BF)

    pick_own, pick_other = picks(c), picks(1 - c)
    own_rows = pl.ds(pl.multiple_of(c * 72, 8), 72)
    own_wv.wait()
    for q in range(4):
        group = wv[:, 256 * q : 256 * (q + 1)]
        wvs[:, 128 * q : 128 * (q + 1)] = nt(group, pick_other)
    wvx_copy = send(wvs, wvx.at[own_rows], core)
    for q in range(4):
        group = wv[:, 256 * q : 256 * (q + 1)]
        wvx[own_rows, 128 * q : 128 * (q + 1)] = nt(group, pick_own)
    own_cot.wait()
    cot_copy = send(cotan, cot2, core)

    own_acts.wait()
    own_gain.wait()

    def norm_step(i):
        at = pl.ds(pl.multiple_of(i * 32, 32), 32)
        xf = acts[at, :].astype(F32)
        inv = lax.rsqrt(jnp.mean(xf * xf, axis=-1, keepdims=True) + 1e-06)
        inv_ref[at, :] = inv
        nrm[at, :] = (xf * inv * gain[...].reshape(1, D)).astype(BF)

    loop(8, norm_step)
    nrm_copy = send(nrm, nrm2, core)

    wvx_copy.wait_recv()
    mine = pl.ds(pl.multiple_of(16 * x, 16), 16)
    wvf[me, mine] = wvx[mine, :].astype(BF)
    wvf[me, 64:144] = wvx[64:144].astype(BF)
    vs = Gather(zdev, ydev, wv_shared)
    vs.own()
    vs.direct(0)
    gs.near(gs.direct)
    gs.far(gs.direct)
    ga.near(ga.chunk)
    gb.near(gb.chunk)
    ga.far(ga.chunk)
    gb.far(gb.chunk)
    vs.near(vs.direct)
    vs.far(vs.direct)
    ga.forward(0)
    gb.forward(0)
    gs.finish()
    wo_share = Share(wo_units)
    ga.forward(-1)
    gb.forward(-1)
    ga.forward(1)
    gb.forward(1)
    va = Gather(ydev, zdev, wv_block(slot_yz, 64, 48))
    vb = Gather(zdev, ydev, wv_block(slot_zy, 112, 32))

    def turn_step(src, at):
        def body(t):
            lanes = pl.ds(pl.multiple_of(t * 256, 256), 256)
            nrmt[lanes, at * 256 : (at + 1) * 256] = src[:, lanes].T

        return body

    loop(9, turn_step(nrm, 0))
    ga.forward(2)
    gb.forward(2)
    va.own()
    vb.own()
    va.chunk(0)
    vb.chunk(0)
    wo_share.forward()
    vs.finish()
    wv_share = Share(wv_units)
    nrm_copy.wait_recv()
    loop(9, turn_step(nrm2, 1))
    va.near(va.chunk)
    vb.near(vb.chunk)
    va.far(va.chunk)
    vb.far(vb.chunk)
    cot_copy.wait_recv()
    ga.finish()
    gb.finish()
    wo_share.rest.wait()

    ri = lax.broadcasted_iota(jnp.int32, (TOK, TOK), 0)
    ci = lax.broadcasted_iota(jnp.int32, (TOK, TOK), 1)
    lower = (ri >= ci).astype(BF)
    upper = (ci >= ri).astype(BF)
    per_count = 1.0 / (lax.broadcasted_iota(jnp.int32, (TOK, 1), 0) + 1).astype(F32)

    for s, cot in enumerate((cotan, cot2)):

        def dmix_step(n, cot=cot, s=s):
            at = pl.ds(pl.multiple_of(n * 256, 256), 256)
            d = nt(cot[...], wof[pl.ds(8 * n, 8)].reshape(256, D))
            dmix[:, at] = (d * per_count).astype(BF)

        loop(2, dmix_step)
        dval[256 * s : 256 * (s + 1), :] = nn(upper, dmix[...]).astype(BF)
        va.forward((0, -1)[s])
        vb.forward((0, -1)[s])

    def gv_half(p):
        def body(t):
            at = pl.ds(pl.multiple_of(t * 576, 16), 576)
            g = nn(nrmt[at, :], dval[:, 256 * p : 256 * (p + 1)]).astype(BF)
            for h in range(2):
                block = g[:, 128 * h : 128 * (h + 1)].reshape(4, 144, 128)
                for k in range(3):
                    gv.bufs[k][0][2 * p + h, t] = block[:, 48 * k : 48 * (k + 1)]

        return body

    loop(4, gv_half(0))
    va.forward(1)
    vb.forward(1)
    wv_share.forward()
    va.forward(2)
    vb.forward(2)
    loop(4, gv_half(1))
    gv.open_rings()
    va.finish()
    vb.finish()
    wv_share.rest.wait()

    for s, nr in enumerate((nrm, nrm2)):
        vals[...] = nn(nr[...], wvf[...].reshape(D, HALF_K)).astype(BF)
        mixed = (nn(lower, vals[...]) * per_count).astype(BF)
        mix_t[:, 256 * s : 256 * (s + 1)] = mixed.T
    for m in range(16):
        for u in range(2):
            mix_tb[256 * u + 16 * m : 256 * u + 16 * (m + 1), :] = mix_t[32 * m + 16 * u : 32 * m + 16 * (u + 1), :]
    for s in (2, 1, -1, 0):
        d = at4(x, s)
        at = pl.ds(pl.multiple_of(256 * (d // 2), 256), 256)
        lanes = pl.ds(pl.multiple_of(HALF_D * (d % 2), 128), HALF_D)
        g = nn(mix_tb[at, :256], cotan[:, lanes]) + nn(mix_tb[at, 256:], cot2[:, lanes])
        g = g.astype(BF).reshape(4, 4, 16, HALF_D)
        for k in range(3):
            go.bufs[k][0][d] = g[:, :, :, 384 * k : 384 * (k + 1)]
        if s != 0:
            go.open_x(s)
        go.open_yz(pl.ds(d, 1))

    for p in range(3):
        gv.sums[p].turn()

    for s in (1, 0):

        def dn_step(g, s=s):
            w = wvf[pl.ds(8 * g, 8)].reshape(D // 2, HALF_K)
            d = nt(dval[256 * s : 256 * (s + 1), :], w)
            at = pl.ds(pl.multiple_of(g * HALF_D, 128), HALF_D)
            if s == 1:
                dn_send[:, at] = d.astype(BF)
            else:
                dn_own[:, at] = d

        loop(2, dn_step)
        if s == 1:
            dn_copy = send(dn_send, dn_recv, core)
    dn_copy.wait_recv()

    def ga_step(i):
        at = pl.ds(pl.multiple_of(i * 32, 32), 32)
        xf, inv = acts[at, :].astype(F32), inv_ref[at, :]
        scaled = gain[...].reshape(1, D) * (dn_own[at, :] + dn_recv[at, :].astype(F32))
        moment = jnp.mean(scaled * xf, axis=-1, keepdims=True)
        out = cotan[at, :].astype(F32) + inv * scaled - xf * (inv * inv * inv * moment)
        ga_out[at, :] = out.astype(BF)

    loop(8, ga_step)
    for p in range(3):
        gv.second(p)
    for p in range(3):
        go.second(p)
    for p in range(3):
        gv.third(p)

    for p in range(3):
        go.third(p)
    cw, ct = Group(), Group()
    for p in range(3):
        part, land = gvw.at[pl.ds(48 * p, 48)], gvw2.at[pl.ds(48 * p, 48)]
        gv.sums[p].close(part)
        send(part, land, zdev(4), cw)
    for p in range(3):
        part, land = got.at[:, pl.ds(384 * p, 384)], got2.at[:, pl.ds(384 * p, 384)]
        go.sums[p].close(part)
        send(part, land, zdev(4), ct)
    cw.wait()
    total = gvw[...].astype(F32) + gvw2[...].astype(F32)
    for h in range(2):
        fin[h, c, x, 0:72] = total[72 * h : 72 * (h + 1)].astype(BF)
    keep, give = fin.at[c, c, x], fin.at[1 - c, c, x]
    cv = Group()
    for s in (1, -1, 2):
        send(keep, keep, xdev(s), cv)
    for s in (0, 1, -1, 2):
        send(give, give, dev(dx=s, dc=1), cv)
    ct.wait()
    gof[x] = (got[...].astype(F32) + got2[...].astype(F32)).astype(BF)
    co = Group()
    for s in (1, -1, 2):
        send(gof.at[x], gof.at[x], xdev(s), co)
    cv.wait()
    pick = [picks(0), picks(1)]
    for q in range(4):
        g = nn(fin[c, 0, q], pick[0]) + nn(fin[c, 1, q], pick[1])
        gv_out[:, 256 * q : 256 * (q + 1)] = g[0:72]
    for k, n in enumerate(out_bytes):
        if k < len(out_bytes) - 1:
            await_bytes(n, ssem.at[k])
    co.wait()
    for u in range(2):
        for h in range(2):
            go_out[16 * u : 16 * (u + 1), HALF_D * h : HALF_D * (h + 1)] = gof[2 * u + h].astype(F32)
    await_bytes(out_bytes[-1], ssem.at[len(out_bytes) - 1])
    assert len(out_bytes) <= N_OUT and in_count[0] <= N_IN, (len(out_bytes), in_count)


def bf(*shape):
    return pltpu.VMEM(shape, BF)


def fl(*shape):
    return pltpu.VMEM(shape, F32)


INPUTS = dict(
    acts=bf(TOK, D), wv=bf(72, KVW), cotan=bf(TOK, D), gain=fl(D), cot2=bf(TOK, D), nrm=bf(TOK, D), nrm2=bf(TOK, D),
    nrmt=bf(D, 2 * TOK), inv=fl(TOK, 1), wof=bf(16, 32, D),
    wvf=bf(16, 144, HALF_K), wvx=fl(144, HALF_K), wvs=fl(72, HALF_K),
)
WORK = dict(
    dmix=bf(TOK, HALF_K), dval=bf(2 * TOK, HALF_K), vals=bf(TOK, HALF_K), mix_t=bf(HALF_K, 2 * TOK),
    mix_tb=bf(HALF_K, 2 * TOK), dn_own=fl(TOK, D), dn_send=bf(TOK, D), dn_recv=bf(TOK, D),
    tally=bf(TALLY, 128),
)
LAST = dict(
    gvw=bf(144, 128), gvw2=bf(144, 128), fin=bf(2, 2, 4, 80, 128),
    got=bf(16, HALF_D), got2=bf(16, HALF_D), gof=bf(4, 16, HALF_D),
    ssem=pltpu.SemaphoreType.DMA((N_OUT,)), rsem=pltpu.SemaphoreType.DMA((N_IN,)),
    lsem=pltpu.SemaphoreType.DMA((6,)),
)
PART = ("terms", "l1", "r1", "m1", "d1", "l2", "r2", "m2", "d2", "l3", "r3", "m3")
LEAD = ((4, 4, 4), (4, 4), (4, 4), (4, 4), (4, 4), (4,), (4,), (4,), (4,), (), (), ())
SCRATCH = dict(INPUTS, **WORK, **LAST)
for name, block in (("gv", (48, 128)), ("go", (16, 384))):
    for p in range(3):
        SCRATCH.update({f"{name}{p}_{n}": bf(*lead, *block) for n, lead in zip(PART, LEAD)})
        if name == "gv":
            SCRATCH.update({f"gv{p}_f{h}": bf(2, 4, *block) for h in range(2)})


def store(*refs):
    copies = [pltpu.make_async_copy(refs[k], refs[3 + k], refs[6].at[k]) for k in range(3)]
    for copy in copies:
        copy.start()
    for copy in copies:
        copy.wait()


def local(acts, value_weight, out_weight, norm_gain, cotan):
    vmem = pl.BlockSpec(memory_space=pltpu.VMEM)
    anywhere = pl.BlockSpec(memory_space=pl.ANY)
    hbm = pl.BlockSpec(memory_space=pltpu.HBM)
    shapes = (
        jax.ShapeDtypeStruct((72, KVW), F32),
        jax.ShapeDtypeStruct((32, D), F32),
        jax.ShapeDtypeStruct((TOK, D), BF),
    )
    acts, value_weight, out_weight, norm_gain, cotan = (
        pltpu.with_memory_space_constraint(a, pltpu.HBM)
        for a in (acts, value_weight, out_weight, norm_gain, cotan)
    )
    outs = pl.pallas_call(
        kernel,
        out_shape=tuple(pltpu.VMEM(shape.shape, shape.dtype) for shape in shapes),
        in_specs=[hbm] * 5,
        out_specs=(vmem, vmem, vmem),
        scratch_shapes=list(SCRATCH.values()),
        name="fused",
        compiler_params=pltpu.CompilerParams(
            collective_id=0, has_side_effects=True, vmem_limit_bytes=48 * 2**20
        ),
    )(acts, value_weight, out_weight, norm_gain, cotan)
    return pl.pallas_call(
        store,
        out_shape=shapes,
        in_specs=[vmem] * 3,
        out_specs=(anywhere,) * 3,
        scratch_shapes=[pltpu.SemaphoreType.DMA((3,))],
        name="store",
    )(*(pltpu.with_memory_space_constraint(out, pltpu.VMEM) for out in outs))


def solution(mesh):
    placed = (
        P(("replica", "fsdp"), None),
        P("fsdp", None),
        P("fsdp", None),
        P(),
        P(("replica", "fsdp"), None),
    )
    return jax.shard_map(
        local,
        mesh=mesh,
        in_specs=placed,
        out_specs=(P("fsdp", None), P("fsdp", None), P(("replica", "fsdp"), None)),
        check_vma=False,
    )
```

```python
import math

import jax
import jax.numpy as jnp
from jax import lax
from jax.experimental import pallas as pl
from jax.experimental.pallas import tpu as pltpu
from jax.sharding import PartitionSpec as P

MESH = pl.DeviceIdType.MESH
BF, F32 = jnp.bfloat16, jnp.float32
D, KVW, TOK = 2304, 1024, 256
HALF_D, HALF_K = D // 2, KVW // 2
N_OUT, N_IN = 7, 94
TALLY = 9216


def nt(a, b):
    return lax.dot_general(a, b, (((1,), (1,)), ((), ())), preferred_element_type=F32)


def nn(a, b):
    return jnp.dot(a, b, preferred_element_type=F32)


def loop(n, body):
    def step(i, carry):
        body(i)
        return carry

    lax.fori_loop(0, n, step, 0)


def rows(ref, start, size):
    return ref.at[pl.ds(pl.multiple_of(start, 16), size)]


def kernel(*refs):
    ref = dict(zip(("acts_in", "wv_in", "wo_in", "gain_in", "cot_in", "gv_out", "go_out", "ga_out", *SCRATCH), refs))
    acts_in, wv_in, wo_in, gain_in, cot_in = (ref[n] for n in ("acts_in", "wv_in", "wo_in", "gain_in", "cot_in"))
    gv_out, go_out, ga_out = (ref[n] for n in ("gv_out", "go_out", "ga_out"))
    acts, wv, cotan, gain, cot2, nrm, nrm2, nrmt, inv_ref, wof, wvf, wvx, wvs = (ref[n] for n in INPUTS)
    dmix, dval, vals, mix_t, mix_tb, dn_own, dn_send, dn_recv, tally = (ref[n] for n in WORK)
    gvw, gvw2, fin, got, got2, gof, ssem, rsem, lsem = (ref[n] for n in LAST)
    r, f = lax.axis_index("replica"), lax.axis_index("fsdp")
    x, y, zl, c = r // 2, f // 8, (f // 2) % 4, f % 2
    z = (r % 2) * 4 + zl
    me = y * 4 + zl

    def dev(dx=0, dy=0, dz=0, dc=0):
        xx, yy, zz, cc = (x + dx + 4) % 4, (y + dy + 4) % 4, (z + dz + 8) % 8, (c + dc) % 2
        return (xx * 2 + zz // 4, yy * 8 + (zz % 4) * 2 + cc)

    def ydev(s):
        return dev(dy=s)

    def zdev(s):
        return dev(dz=s)

    def xdev(s):
        return dev(dx=s)

    def at4(q, s):
        return (q + s + 4) % 4

    core = dev(dc=1)
    partners = [core, *(xdev(s) for s in (1, -1, 2)), *(dev(dx=s, dc=1) for s in (1, -1, 2))]
    partners += [*(ydev(s) for s in (1, -1, 2)), *(zdev(s) for s in (1, -1, 2, -2, 4))]
    barrier = pltpu.get_barrier_semaphore()
    for p in partners:
        pl.semaphore_signal(barrier, inc=1, device_id=p, device_id_type=MESH)

    own_unit = pl.ds(pl.multiple_of(128 * x, 128), 128)
    own_wo = [
        pltpu.make_async_copy(wo_in.at[:, cols], wof.at[me, :, cols], lsem.at[h])
        for h, cols in enumerate((own_unit, pl.ds(512, D - 512)))
    ]
    own_wv = pltpu.make_async_copy(wv_in, wv, lsem.at[2])
    own_cot = pltpu.make_async_copy(cot_in, cotan, lsem.at[3])
    own_acts = pltpu.make_async_copy(acts_in, acts, lsem.at[4])
    own_gain = pltpu.make_async_copy(gain_in, gain, lsem.at[5])
    for copy in (*own_wo, own_wv, own_cot, own_acts, own_gain):
        copy.start()

    pl.semaphore_wait(barrier, len(partners))

    def await_bytes(n, sem):
        view = tally.at[pl.ds(0, n // 256)]
        pltpu.make_async_copy(view, view, sem).wait()

    out_bytes, in_count = [0], [0]

    class Group:
        def __init__(self):
            self.i, self.bytes = in_count[0], 0
            in_count[0] += 1

        def wait(self):
            await_bytes(self.bytes, rsem.at[self.i])

    def send(src, dst, to, group=None):
        n = math.prod(src.shape) * jnp.dtype(src.dtype).itemsize
        if out_bytes[-1] + n > TALLY * 256:
            out_bytes.append(0)
        out_bytes[-1] += n
        alone = group is None
        group = Group() if alone else group
        group.bytes += n
        copy = pltpu.make_async_remote_copy(
            src_ref=src, dst_ref=dst, send_sem=ssem.at[len(out_bytes) - 1], recv_sem=rsem.at[group.i],
            device_id=to, device_id_type=MESH,
        )
        copy.start()
        return copy if alone else None

    class Gather:
        def __init__(self, first, second, block):
            self.first, self.second, self.block = first, second, block
            self.p2, self.rest = {}, Group()

        def spread(self, to, block, near, far):
            b = block(None)
            copies = (send(b, b, to(1), near), send(b, b, to(-1), near))
            if to is zdev:
                h0, h1 = block(0), block(1)
                send(h0, h0, to(2), far)
                send(h1, h1, to(-2), far)
            else:
                send(b, b, to(2), far)
            return copies

        def own(self):
            self.p1far = Group()
            self.p1 = self.spread(self.first, lambda h: self.block(0, 0, h), None, self.p1far)

        def chunk(self, i):
            b = self.block(i, 0, None)
            self.p2[i] = (send(b, b, self.second(1)), send(b, b, self.second(-1)))

        def direct(self, i):
            self.spread(self.second, lambda h: self.block(i, 0, h), self.rest, self.rest)

        def near(self, then):
            self.p1[0].wait_recv()
            then(-1)
            self.p1[1].wait_recv()
            then(1)

        def far(self, then):
            self.p1far.wait()
            then(2)

        def forward(self, i):
            up, down = self.p2[i]
            up.wait_recv()
            b = self.block(i, -1, 0)
            send(b, b, self.second(1), self.rest)
            down.wait_recv()
            b = self.block(i, 1, 1)
            send(b, b, self.second(-1), self.rest)

        def finish(self):
            self.rest.wait()

    def slot_yz(i, j):
        return at4(y, i) * 4 + at4(zl, j)

    def slot_zy(i, j):
        return at4(y, j) * 4 + at4(zl, i)

    def wo_block(slot, lo, n):
        def block(i, j, half):
            at = wof.at[slot(i, j), :, pl.ds(lo, n)]
            return at if half is None else at.at[pl.ds(16 * half, 16)]

        return block

    def wo_shared(i, j, half):
        at = wof.at[slot_yz(i, j), :, own_unit]
        return at if half is None else at.at[pl.ds(16 * half, 16)]

    def wv_block(slot, lo, n):
        def block(i, j, half):
            at = wvf.at[slot(i, j), pl.ds(lo, n)]
            return at if half is None else at.at[:, pl.ds(256 * half, 256)]

        return block

    def wv_shared(i, j, half):
        at = wvf.at[slot_zy(i, j), pl.ds(pl.multiple_of(16 * x, 16), 16)]
        return at if half is None else at.at[:, pl.ds(256 * half, 256)]

    class Sum:
        def __init__(self, own, left, right, far):
            self.own, self.left, self.right, self.far = own, left, right, far
            self.group = Group()

        def close(self, out):
            self.group.wait()
            total = self.own[...].astype(F32) + self.left[...].astype(F32)
            total += self.right[...].astype(F32) + self.far[...].astype(F32)
            out[...] = total.astype(BF)

    def direct(to, part, left, right, far, halves):
        got_sum = Sum(part(0), left, right, far)
        send(part(1), left, to(1), got_sum.group)
        send(part(-1), right, to(-1), got_sum.group)
        p = part(2)
        if to is zdev:
            for h, hop in enumerate((2, -2)):
                send(halves(p, h), halves(far, h), to(hop), got_sum.group)
        else:
            send(p, far, to(2), got_sum.group)
        return got_sum

    def two(p, h):
        return p.at[pl.ds(2 * h, 2)]

    class Ring:
        def __init__(self, to, part, f0, f1, left, right):
            self.to, self.part = to, part
            self.f0, self.f1, self.left, self.right = f0, f1, left, right

        def recv(self, ref, h):
            return ref.at[pl.ds(2 * h, 2)]

        def open(self):
            self.rest = Group()
            self.c0 = send(self.part(2, 0), self.f0, self.to(1))
            self.c1 = send(self.part(2, 1), self.f1, self.to(-1))
            send(self.part(1, 1), self.recv(self.left, 1), self.to(1), self.rest)
            send(self.part(-1, 0), self.recv(self.right, 0), self.to(-1), self.rest)

        def turn(self):
            self.c0.wait_recv()
            h = self.part(1, 0)
            h[...] = (h[...].astype(F32) + self.f0[...].astype(F32)).astype(BF)
            send(h, self.recv(self.left, 0), self.to(1), self.rest)
            self.c1.wait_recv()
            h = self.part(-1, 1)
            h[...] = (h[...].astype(F32) + self.f1[...].astype(F32)).astype(BF)
            send(h, self.recv(self.right, 1), self.to(-1), self.rest)

        def close(self, out):
            self.rest.wait()
            for h in range(2):
                total = self.part(0, h)[...].astype(F32) + self.recv(self.left, h)[...].astype(F32)
                total += self.recv(self.right, h)[...].astype(F32)
                o = self.recv(out, h)
                o[...] = total.astype(BF)

    class Reduce:
        def __init__(self, name, halves):
            self.bufs = [[ref[f"{name}{p}_{n}"] for n in PART] for p in range(3)]
            self.halves = halves
            bx, by, bz = (b[0] for b in self.bufs)
            own = (bx.at[x], by.at[:, y], bz.at[:, :, zl])
            self.sums = [Sum(own[p], *self.bufs[p][1:4]) if name == "go" else None for p in range(3)]

        def open_rings(self):
            bx, by, bz = (b[0] for b in self.bufs)
            parts = (
                (xdev, lambda s, h: bx.at[at4(x, s), pl.ds(2 * h, 2)]),
                (ydev, lambda s, h: by.at[pl.ds(2 * h, 2), at4(y, s)]),
                (zdev, lambda s, h: bz.at[pl.ds(2 * h, 2), :, at4(zl, s)]),
            )
            for p in range(3):
                self.sums[p] = Ring(*parts[p], ref[f"gv{p}_f0"], ref[f"gv{p}_f1"], *self.bufs[p][1:3])
                self.sums[p].open()

        def open_x(self, s):
            land = {1: 1, -1: 2, 2: 3}[s]
            send(self.bufs[0][0].at[at4(x, s)], self.bufs[0][land], xdev(s), self.sums[0].group)

        def open_yz(self, units):
            by, lefty, righty, fary = self.bufs[1][:4]
            bz, leftz, rightz, farz = self.bufs[2][:4]
            for s, land in ((2, fary), (1, lefty), (-1, righty)):
                send(by.at[units, at4(y, s)], land.at[units], ydev(s), self.sums[1].group)
            for h, hop in enumerate((2, -2)):
                at = pl.ds(2 * h, 2)
                send(bz.at[units, at, at4(zl, 2)], farz.at[units, at], zdev(hop), self.sums[2].group)
            for s, land in ((1, leftz), (-1, rightz)):
                send(bz.at[units, :, at4(zl, s)], land.at[units], zdev(s), self.sums[2].group)

        def second(self, p):
            done = self.bufs[p][4]
            self.sums[p].close(done)
            to, part = (
                (ydev, lambda s: done.at[at4(y, s)]),
                (zdev, lambda s: done.at[:, at4(zl, s)]),
                (xdev, lambda s: done.at[at4(x, s)]),
            )[p]
            self.sums[p] = direct(to, part, *self.bufs[p][5:8], two)

        def third(self, p):
            done = self.bufs[p][8]
            self.sums[p].close(done)
            to, q = ((zdev, zl), (xdev, x), (ydev, y))[p]
            self.sums[p] = direct(to, lambda s: done.at[at4(q, s)], *self.bufs[p][9:12], self.halves)

    gv = Reduce("gv", lambda p, h: p.at[pl.ds(32 * h, 32 - 16 * h)])
    go = Reduce("go", lambda p, h: p.at[:, pl.ds(256 * h, 256 - 128 * h)])

    class Share:
        def __init__(self, pick):
            self.pick, self.rest = pick, Group()
            p = pick(0, pl.ds(0, 16))
            self.up, self.down = send(p, p, xdev(1)), send(p, p, xdev(-1))

        def forward(self):
            self.up.wait_recv()
            p = self.pick(-1, pl.ds(0, 8))
            send(p, p, xdev(1), self.rest)
            self.down.wait_recv()
            p = self.pick(1, pl.ds(8, 8))
            send(p, p, xdev(-1), self.rest)

    def wo_units(s, blocks):
        return wof.at[blocks, :, pl.ds(pl.multiple_of(128 * at4(x, s), 128), 128)]

    def wv_units(s, blocks):
        return wvf.at[blocks, pl.ds(pl.multiple_of(16 * at4(x, s), 16), 16)]

    gs = Gather(ydev, zdev, wo_shared)
    ga = Gather(ydev, zdev, wo_block(slot_yz, 512, 896))
    gb = Gather(zdev, ydev, wo_block(slot_zy, 1408, 896))
    for copy in own_wo:
        copy.wait()
    gs.own()
    gs.direct(0)
    ga.own()
    gb.own()
    ga.chunk(0)
    gb.chunk(0)

    jj = lax.broadcasted_iota(jnp.int32, (128, 256), 0)
    kk = lax.broadcasted_iota(jnp.int32, (128, 256), 1)
    base = 64 * (jj // 32) + jj % 32

    def picks(which):
        return (kk == base + 32 * which).astype(BF)

    pick_own, pick_other = picks(c), picks(1 - c)
    own_rows = pl.ds(pl.multiple_of(c * 72, 8), 72)
    own_wv.wait()
    for q in range(4):
        group = wv[:, 256 * q : 256 * (q + 1)]
        wvs[:, 128 * q : 128 * (q + 1)] = nt(group, pick_other)
    wvx_copy = send(wvs, wvx.at[own_rows], core)
    for q in range(4):
        group = wv[:, 256 * q : 256 * (q + 1)]
        wvx[own_rows, 128 * q : 128 * (q + 1)] = nt(group, pick_own)
    own_cot.wait()
    cot_copy = send(cotan, cot2, core)

    own_acts.wait()
    own_gain.wait()

    def norm_step(i):
        at = pl.ds(pl.multiple_of(i * 32, 32), 32)
        xf = acts[at, :].astype(F32)
        inv = lax.rsqrt(jnp.mean(xf * xf, axis=-1, keepdims=True) + 1e-06)
        inv_ref[at, :] = inv
        nrm[at, :] = (xf * inv * gain[...].reshape(1, D)).astype(BF)

    loop(8, norm_step)
    nrm_copy = send(nrm, nrm2, core)

    wvx_copy.wait_recv()
    mine = pl.ds(pl.multiple_of(16 * x, 16), 16)
    wvf[me, mine] = wvx[mine, :].astype(BF)
    wvf[me, 64:144] = wvx[64:144].astype(BF)
    vs = Gather(zdev, ydev, wv_shared)
    vs.own()
    vs.direct(0)
    gs.near(gs.direct)
    gs.far(gs.direct)
    ga.near(ga.chunk)
    gb.near(gb.chunk)
    ga.far(ga.chunk)
    gb.far(gb.chunk)
    vs.near(vs.direct)
    vs.far(vs.direct)
    ga.forward(0)
    gb.forward(0)
    gs.finish()
    wo_share = Share(wo_units)
    ga.forward(-1)
    gb.forward(-1)
    ga.forward(1)
    gb.forward(1)
    va = Gather(ydev, zdev, wv_block(slot_yz, 64, 48))
    vb = Gather(zdev, ydev, wv_block(slot_zy, 112, 32))

    def turn_step(src, at):
        def body(t):
            lanes = pl.ds(pl.multiple_of(t * 256, 256), 256)
            nrmt[lanes, at * 256 : (at + 1) * 256] = src[:, lanes].T

        return body

    loop(9, turn_step(nrm, 0))
    ga.forward(2)
    gb.forward(2)
    va.own()
    vb.own()
    va.chunk(0)
    vb.chunk(0)
    wo_share.forward()
    vs.finish()
    wv_share = Share(wv_units)
    nrm_copy.wait_recv()
    loop(9, turn_step(nrm2, 1))
    va.near(va.chunk)
    vb.near(vb.chunk)
    va.far(va.chunk)
    vb.far(vb.chunk)
    cot_copy.wait_recv()
    ga.finish()
    gb.finish()
    wo_share.rest.wait()

    ri = lax.broadcasted_iota(jnp.int32, (TOK, TOK), 0)
    ci = lax.broadcasted_iota(jnp.int32, (TOK, TOK), 1)
    lower = (ri >= ci).astype(BF)
    upper = (ci >= ri).astype(BF)
    per_count = 1.0 / (lax.broadcasted_iota(jnp.int32, (TOK, 1), 0) + 1).astype(F32)

    for s, cot in enumerate((cotan, cot2)):

        def dmix_step(n, cot=cot, s=s):
            at = pl.ds(pl.multiple_of(n * 256, 256), 256)
            d = nt(cot[...], wof[pl.ds(8 * n, 8)].reshape(256, D))
            dmix[:, at] = (d * per_count).astype(BF)

        loop(2, dmix_step)
        dval[256 * s : 256 * (s + 1), :] = nn(upper, dmix[...]).astype(BF)
        va.forward((0, -1)[s])
        vb.forward((0, -1)[s])

    def gv_half(p):
        def body(t):
            at = pl.ds(pl.multiple_of(t * 576, 16), 576)
            g = nn(nrmt[at, :], dval[:, 256 * p : 256 * (p + 1)]).astype(BF)
            for h in range(2):
                block = g[:, 128 * h : 128 * (h + 1)].reshape(4, 144, 128)
                for k in range(3):
                    gv.bufs[k][0][2 * p + h, t] = block[:, 48 * k : 48 * (k + 1)]

        return body

    loop(4, gv_half(0))
    va.forward(1)
    vb.forward(1)
    wv_share.forward()
    va.forward(2)
    vb.forward(2)
    loop(4, gv_half(1))
    gv.open_rings()
    va.finish()
    vb.finish()
    wv_share.rest.wait()

    for s, nr in enumerate((nrm, nrm2)):
        vals[...] = nn(nr[...], wvf[...].reshape(D, HALF_K)).astype(BF)
        mixed = (nn(lower, vals[...]) * per_count).astype(BF)
        mix_t[:, 256 * s : 256 * (s + 1)] = mixed.T
    for m in range(16):
        for u in range(2):
            mix_tb[256 * u + 16 * m : 256 * u + 16 * (m + 1), :] = mix_t[32 * m + 16 * u : 32 * m + 16 * (u + 1), :]
    for s in (2, 1, -1, 0):
        d = at4(x, s)
        at = pl.ds(pl.multiple_of(256 * (d // 2), 256), 256)
        lanes = pl.ds(pl.multiple_of(HALF_D * (d % 2), 128), HALF_D)
        g = nn(mix_tb[at, :256], cotan[:, lanes]) + nn(mix_tb[at, 256:], cot2[:, lanes])
        g = g.astype(BF).reshape(4, 4, 16, HALF_D)
        for k in range(3):
            go.bufs[k][0][d] = g[:, :, :, 384 * k : 384 * (k + 1)]
        if s != 0:
            go.open_x(s)
        go.open_yz(pl.ds(d, 1))

    for p in range(3):
        gv.sums[p].turn()

    for s in (1, 0):

        def dn_step(g, s=s):
            w = wvf[pl.ds(8 * g, 8)].reshape(D // 2, HALF_K)
            d = nt(dval[256 * s : 256 * (s + 1), :], w)
            at = pl.ds(pl.multiple_of(g * HALF_D, 128), HALF_D)
            if s == 1:
                dn_send[:, at] = d.astype(BF)
            else:
                dn_own[:, at] = d

        loop(2, dn_step)
        if s == 1:
            dn_copy = send(dn_send, dn_recv, core)
    dn_copy.wait_recv()

    def ga_step(i):
        at = pl.ds(pl.multiple_of(i * 32, 32), 32)
        xf, inv = acts[at, :].astype(F32), inv_ref[at, :]
        scaled = gain[...].reshape(1, D) * (dn_own[at, :] + dn_recv[at, :].astype(F32))
        moment = jnp.mean(scaled * xf, axis=-1, keepdims=True)
        out = cotan[at, :].astype(F32) + inv * scaled - xf * (inv * inv * inv * moment)
        ga_out[at, :] = out.astype(BF)

    loop(8, ga_step)
    for p in range(3):
        gv.second(p)
    for p in range(3):
        go.second(p)
    for p in range(3):
        gv.third(p)

    for p in range(3):
        go.third(p)
    cw, ct = Group(), Group()
    for p in range(3):
        part, land = gvw.at[pl.ds(48 * p, 48)], gvw2.at[pl.ds(48 * p, 48)]
        gv.sums[p].close(part)
        send(part, land, zdev(4), cw)
    for p in range(3):
        part, land = got.at[:, pl.ds(384 * p, 384)], got2.at[:, pl.ds(384 * p, 384)]
        go.sums[p].close(part)
        send(part, land, zdev(4), ct)
    cw.wait()
    total = gvw[...].astype(F32) + gvw2[...].astype(F32)
    for h in range(2):
        fin[h, c, x, 0:72] = total[72 * h : 72 * (h + 1)].astype(BF)
    keep, give = fin.at[c, c, x], fin.at[1 - c, c, x]
    cv = Group()
    for s in (1, -1, 2):
        send(keep, keep, xdev(s), cv)
    for s in (0, 1, -1, 2):
        send(give, give, dev(dx=s, dc=1), cv)
    ct.wait()
    gof[x] = (got[...].astype(F32) + got2[...].astype(F32)).astype(BF)
    co = Group()
    for s in (1, -1, 2):
        send(gof.at[x], gof.at[x], xdev(s), co)
    cv.wait()
    pick = [picks(0), picks(1)]
    for q in range(4):
        g = nn(fin[c, 0, q], pick[0]) + nn(fin[c, 1, q], pick[1])
        gv_out[:, 256 * q : 256 * (q + 1)] = g[0:72]
    for k, n in enumerate(out_bytes):
        if k < len(out_bytes) - 1:
            await_bytes(n, ssem.at[k])
    co.wait()
    for u in range(2):
        for h in range(2):
            go_out[16 * u : 16 * (u + 1), HALF_D * h : HALF_D * (h + 1)] = gof[2 * u + h].astype(F32)
    await_bytes(out_bytes[-1], ssem.at[len(out_bytes) - 1])
    assert len(out_bytes) <= N_OUT and in_count[0] <= N_IN, (len(out_bytes), in_count)


def bf(*shape):
    return pltpu.VMEM(shape, BF)


def fl(*shape):
    return pltpu.VMEM(shape, F32)


INPUTS = dict(
    acts=bf(TOK, D), wv=bf(72, KVW), cotan=bf(TOK, D), gain=fl(D), cot2=bf(TOK, D), nrm=bf(TOK, D), nrm2=bf(TOK, D),
    nrmt=bf(D, 2 * TOK), inv=fl(TOK, 1), wof=bf(16, 32, D),
    wvf=bf(16, 144, HALF_K), wvx=fl(144, HALF_K), wvs=fl(72, HALF_K),
)
WORK = dict(
    dmix=bf(TOK, HALF_K), dval=bf(2 * TOK, HALF_K), vals=bf(TOK, HALF_K), mix_t=bf(HALF_K, 2 * TOK),
    mix_tb=bf(HALF_K, 2 * TOK), dn_own=fl(TOK, D), dn_send=bf(TOK, D), dn_recv=bf(TOK, D),
    tally=bf(TALLY, 128),
)
LAST = dict(
    gvw=bf(144, 128), gvw2=bf(144, 128), fin=bf(2, 2, 4, 80, 128),
    got=bf(16, HALF_D), got2=bf(16, HALF_D), gof=bf(4, 16, HALF_D),
    ssem=pltpu.SemaphoreType.DMA((N_OUT,)), rsem=pltpu.SemaphoreType.DMA((N_IN,)),
    lsem=pltpu.SemaphoreType.DMA((6,)),
)
PART = ("terms", "l1", "r1", "m1", "d1", "l2", "r2", "m2", "d2", "l3", "r3", "m3")
LEAD = ((4, 4, 4), (4, 4), (4, 4), (4, 4), (4, 4), (4,), (4,), (4,), (4,), (), (), ())
SCRATCH = dict(INPUTS, **WORK, **LAST)
for name, block in (("gv", (48, 128)), ("go", (16, 384))):
    for p in range(3):
        SCRATCH.update({f"{name}{p}_{n}": bf(*lead, *block) for n, lead in zip(PART, LEAD)})
        if name == "gv":
            SCRATCH.update({f"gv{p}_f{h}": bf(2, 4, *block) for h in range(2)})


def store(*refs):
    copies = [pltpu.make_async_copy(refs[k], refs[3 + k], refs[6].at[k]) for k in range(3)]
    for copy in copies:
        copy.start()
    for copy in copies:
        copy.wait()


def local(acts, value_weight, out_weight, norm_gain, cotan):
    vmem = pl.BlockSpec(memory_space=pltpu.VMEM)
    anywhere = pl.BlockSpec(memory_space=pl.ANY)
    hbm = pl.BlockSpec(memory_space=pltpu.HBM)
    shapes = (
        jax.ShapeDtypeStruct((72, KVW), F32),
        jax.ShapeDtypeStruct((32, D), F32),
        jax.ShapeDtypeStruct((TOK, D), BF),
    )
    acts, value_weight, out_weight, norm_gain, cotan = (
        pltpu.with_memory_space_constraint(a, pltpu.HBM)
        for a in (acts, value_weight, out_weight, norm_gain, cotan)
    )
    outs = pl.pallas_call(
        kernel,
        out_shape=tuple(pltpu.VMEM(shape.shape, shape.dtype) for shape in shapes),
        in_specs=[hbm] * 5,
        out_specs=(vmem, vmem, vmem),
        scratch_shapes=list(SCRATCH.values()),
        name="fused",
        compiler_params=pltpu.CompilerParams(
            collective_id=0, has_side_effects=True, vmem_limit_bytes=48 * 2**20
        ),
    )(acts, value_weight, out_weight, norm_gain, cotan)
    return pl.pallas_call(
        store,
        out_shape=shapes,
        in_specs=[vmem] * 3,
        out_specs=(anywhere,) * 3,
        scratch_shapes=[pltpu.SemaphoreType.DMA((3,))],
        name="store",
    )(*(pltpu.with_memory_space_constraint(out, pltpu.VMEM) for out in outs))


def solution(mesh):
    placed = (
        P(("replica", "fsdp"), None),
        P("fsdp", None),
        P("fsdp", None),
        P(),
        P(("replica", "fsdp"), None),
    )
    return jax.shard_map(
        local,
        mesh=mesh,
        in_specs=placed,
        out_specs=(P("fsdp", None), P("fsdp", None), P(("replica", "fsdp"), None)),
        check_vma=False,
    )
```
